256 devices in a mesh: surf: 32 (over y, z), vol: 8 (over x, core).
Axes of the slice: x: 4, y: 4, z: 8, core: 2. Of those that a mesh axis runs over, the one named last changes fastest.
Arguments:
- centres: float32 [3, 65536], P(None, 'surf'), may hold values from -8 to 40, as said below
- mode_shapes: float32 [16, 65536], P(None, 'surf'), may hold values from -16 to 16
- neighbours: int32 [256, 9], P('surf'), may hold values from -1 to 255, as said below
- volume_nodes: float32 [3, 8388608], P(None, ('surf', 'vol')), may hold values from -8 to 40
- supports: int32 [32768, 9], P(('surf', 'vol')), may hold values from -1 to 255, as said below
Outputs:
- rbf_weights: float32 [16, 65536], P(None, 'surf')
- displacement: float32 [16, 8388608], P(None, ('surf', 'vol'))
The draws below stay inside these ranges and needn't reach their ends.
Inputs may be any that keep to these rules, and one draw needn't show every extreme that they name: `neighbours`: row b lists block b and every block whose surface cell touches its cell, each once; -1 marks an empty slot. A listed id divided by 8 (rounded down) differs from b divided by 8 by at most one. If c is listed in row b, b is listed in row c. `supports`: row t lists distinct block ids first and -1 after them, at least two ids. A listed id divided by 8 differs from t divided by 1024 (both rounded down) by at most one. Some row lists 9 ids. Tiles of lower index along vol tend to list more ids. `centres`: centres of two blocks that are not listed in each other's rows of neighbours are more than 0.9 apart.
All inputs are finite; a program needn't handle non-finite values.
Results may differ from the reference program's by a relative error of at most 0.012.
Values may be sent and summed in bfloat16 or wider, within the bound.
No kernel may reach another device: no remote copies, remote signals or barrier semaphores. Data moves between devices by JAX's collectives and lax.ppermute only.
A program may use at most 128 MiB of HBM per device.

```python
import math
import jax
import jax.numpy as jnp
from jax import lax

MODES = 16
BLK = 256
SLOTS = 9
ITERS = 3
BLK_DEV = 8
T_DEV = 128
NBLK = 256
NS = 65536
NTILES = 32768
NV = 8388608
N_VOL = 8


def strip_layout(key):
    strip_count = NBLK // BLK_DEV
    keys = jax.random.split(jax.random.fold_in(key, 101), strip_count)

    def shuffle(one_key):
        return jax.random.permutation(one_key, BLK_DEV)
    cells = jax.vmap(shuffle)(keys).astype(jnp.int32)
    rows = jnp.broadcast_to(jnp.arange(strip_count, dtype=jnp.int32)[:, None], (strip_count, BLK_DEV))
    locals_ = jnp.broadcast_to(jnp.arange(BLK_DEV, dtype=jnp.int32)[None, :], (strip_count, BLK_DEV))
    blocks = jnp.zeros((strip_count, BLK_DEV), jnp.int32).at[rows, cells].set(locals_)
    return (cells, blocks)


def tile_cells(key):
    return jax.random.randint(jax.random.fold_in(key, 202), (NTILES,), 0, BLK_DEV).astype(jnp.int32)


def touching(blocks, strip_index, cell_index):
    strip_count = blocks.shape[0]
    found = []
    for shift_strip in (-1, 0, 1):
        for shift_cell in (-1, 0, 1):
            other = strip_index + shift_strip
            inside = (other >= 0) & (other < strip_count)
            safe_strip = jnp.clip(other, 0, strip_count - 1)
            column = (cell_index + shift_cell) % BLK_DEV
            ident = safe_strip * BLK_DEV + blocks[safe_strip, column]
            found.append(jnp.where(inside, ident, -1))
    return jnp.stack(found, axis=-1).astype(jnp.int32)


def draw_neighbours(key, part):
    cells, blocks = strip_layout(key)
    ident = jnp.arange(NBLK, dtype=jnp.int32)
    return touching(blocks, ident // BLK_DEV, cells.reshape(-1))


def draw_centres(key, part):
    cells, blocks = strip_layout(key)
    key = jax.random.fold_in(key, 2)
    key_a, key_b, key_c = jax.random.split(key, 3)
    along = jax.random.uniform(key_a, (NBLK, BLK), jnp.float32)
    across = jax.random.uniform(key_b, (NBLK, BLK), jnp.float32)
    bump = 0.05 * jax.random.uniform(key_c, (NBLK, BLK), jnp.float32)
    cell_pos = cells.reshape(-1)[:, None].astype(jnp.float32)
    strip_pos = (jnp.arange(NBLK, dtype=jnp.int32) // BLK_DEV)[:, None].astype(jnp.float32)
    circle = BLK_DEV / (2.0 * math.pi)
    angle = 2.0 * math.pi * (cell_pos + along) / BLK_DEV
    radius = circle * (1.0 + bump)
    stacked = jnp.stack([radius * jnp.cos(angle), strip_pos + across, radius * jnp.sin(angle)])
    return stacked.reshape(3, NS)


def draw_volume_nodes(key, part):
    cells_t = tile_cells(key)
    key = jax.random.fold_in(key, 3)
    key_a, key_b, key_c = jax.random.split(key, 3)
    along = jax.random.uniform(key_a, (NTILES, BLK), jnp.float32)
    across = jax.random.uniform(key_b, (NTILES, BLK), jnp.float32)
    lift = jax.random.uniform(key_c, (NTILES, BLK), jnp.float32)
    ident = jnp.arange(NTILES, dtype=jnp.int32)
    strip_pos = (ident // (T_DEV * N_VOL))[:, None].astype(jnp.float32)
    layer = (ident // T_DEV % N_VOL)[:, None].astype(jnp.float32)
    circle = BLK_DEV / (2.0 * math.pi)
    angle = 2.0 * math.pi * (cells_t[:, None].astype(jnp.float32) + along) / BLK_DEV
    radius = circle + (layer + lift) * 0.5 / N_VOL
    stacked = jnp.stack([radius * jnp.cos(angle), strip_pos + across, radius * jnp.sin(angle)])
    return stacked.reshape(3, NV)


def draw_supports(key, part):
    cells, blocks = strip_layout(key)
    cells_t = tile_cells(key)
    key = jax.random.fold_in(key, 4)
    key_a, key_b, key_c = jax.random.split(key, 3)
    ident = jnp.arange(NTILES, dtype=jnp.int32)
    strip_index = ident // (T_DEV * N_VOL)
    layer = ident // T_DEV % N_VOL
    leading = ident % T_DEV == 0
    candidates = touching(blocks, strip_index, cells_t)

    def shuffle(one_key):
        return jax.random.permutation(one_key, SLOTS)
    order = jax.vmap(shuffle)(jax.random.split(key_a, NTILES)).astype(jnp.int32)
    mixed = jnp.take_along_axis(candidates, order, axis=1)
    ranking = jnp.where(mixed < 0, 100, 0) + jnp.arange(SLOTS, dtype=jnp.int32)[None, :]
    packed = jnp.take_along_axis(mixed, jnp.argsort(ranking, axis=1), axis=1)
    present = jnp.sum((candidates >= 0).astype(jnp.int32), axis=1)
    heavy = jax.random.randint(key_b, (NTILES,), 7, 10)
    light = jax.random.randint(key_c, (NTILES,), 2, 5)
    wanted = jnp.where(layer == 0, heavy, light)
    wanted = jnp.where((layer == 0) & leading, SLOTS, wanted)
    count = jnp.minimum(wanted, present)
    return jnp.where(jnp.arange(SLOTS, dtype=jnp.int32)[None, :] < count[:, None], packed, -1).astype(jnp.int32)


def draw_mode_shapes(key, part):
    key = jax.random.fold_in(key, 5)
    strip_count = NBLK // BLK_DEV
    strip_pos = (jnp.arange(NS, dtype=jnp.int32) // (BLK_DEV * BLK)).astype(jnp.float32)
    growth = 1.0 + 2.0 * strip_pos / (strip_count - 1)
    base = jnp.clip(jax.random.normal(key, (MODES, NS), jnp.float32), -5.0, 5.0)
    return base * growth[None, :]


def setup_inputs(seed: int = 0) -> dict:
    arg_keys = jax.random.split(jax.random.key(seed), 6)
    return {
        "centres": draw_centres(jax.random.fold_in(arg_keys[5], 71), 0),
        "mode_shapes": draw_mode_shapes(jax.random.fold_in(arg_keys[5], 71), 0),
        "neighbours": draw_neighbours(jax.random.fold_in(arg_keys[5], 71), 0),
        "volume_nodes": draw_volume_nodes(jax.random.fold_in(arg_keys[5], 71), 0),
        "supports": draw_supports(jax.random.fold_in(arg_keys[5], 71), 0),
    }


support_radius = 0.9
diag_shift = 0.5
highest = lax.Precision.HIGHEST

def wendland(first_pts, second_pts):
    distance = (first_pts[0] - second_pts[0]) ** 2 + (first_pts[1] - second_pts[1]) ** 2 + (first_pts[2] - second_pts[2]) ** 2
    scaled = jnp.sqrt(distance) / support_radius
    remain = jnp.maximum(1.0 - scaled, 0.0)
    return remain ** 4 * (4.0 * scaled + 1.0)

def operate(vector_field, centres, neighbours):
    block_pts = centres.reshape(3, NBLK, BLK)
    block_vals = vector_field.reshape(MODES, NBLK, BLK)

    def one_block(inputs):
        own_pts, block_ids = inputs
        safe_ids = jnp.maximum(block_ids, 0)
        near_pts = jnp.take(block_pts, safe_ids, axis=1)
        values = jnp.take(block_vals, safe_ids, axis=1)
        kernel = wendland(own_pts[:, None, :, None], near_pts[:, :, None, :]) * (block_ids >= 0)[:, None, None]
        return jnp.einsum('kij,mkj->mi', kernel, values, precision=highest)
    pieces = lax.map(one_block, (jnp.transpose(block_pts, (1, 0, 2)), neighbours))
    return diag_shift * vector_field + jnp.transpose(pieces, (1, 0, 2)).reshape(MODES, NS)

def reference(centres, mode_shapes, neighbours, volume_nodes, supports):
    solution = jnp.zeros_like(mode_shapes)
    residual = mode_shapes
    direction = mode_shapes
    norm_now = lax.optimization_barrier(jnp.sum(residual * residual, axis=1))
    for iteration in range(ITERS):
        applied = operate(direction, centres, neighbours)
        step_size = norm_now / lax.optimization_barrier(jnp.sum(direction * applied, axis=1))
        solution = solution + step_size[:, None] * direction
        residual = residual - step_size[:, None] * applied
        norm_next = lax.optimization_barrier(jnp.sum(residual * residual, axis=1))
        direction = residual + (norm_next / norm_now)[:, None] * direction
        norm_now = norm_next
    weights_low = solution.astype(jnp.bfloat16)
    block_pts = centres.reshape(3, NBLK, BLK)
    block_wts = weights_low.reshape(MODES, NBLK, BLK)

    def one_tile(inputs):
        tile_pts, block_ids = inputs
        count = jnp.sum((block_ids >= 0).astype(jnp.int32))

        def add_slot(slot_index, running):
            ident = jnp.maximum(block_ids[slot_index], 0)
            source = lax.dynamic_index_in_dim(block_pts, ident, 1, keepdims=False)
            weights = lax.dynamic_index_in_dim(block_wts, ident, 1, keepdims=False)
            kernel = wendland(tile_pts[:, :, None], source[:, None, :]).astype(jnp.bfloat16)
            return running + jnp.dot(weights, kernel.T, preferred_element_type=jnp.float32)
        return lax.fori_loop(0, count, add_slot, jnp.zeros((MODES, BLK), jnp.float32))
    tiles_pts = jnp.transpose(volume_nodes.reshape(3, NTILES, BLK), (1, 0, 2))
    moved = lax.map(one_tile, (tiles_pts, supports))
    moved = jnp.transpose(moved, (1, 0, 2)).reshape(MODES, NV)
    power = lax.optimization_barrier(jnp.sum(moved * moved, axis=1))
    scale = jnp.sqrt(power / NV + 1e-06)
    return (solution, moved / scale[:, None])
```

```python
import functools

import jax
import jax.numpy as jnp
from jax import lax
from jax.experimental import pallas as pl
from jax.experimental.pallas import tpu as pltpu
from jax.sharding import PartitionSpec as P

MODES = 16
BLK = 256
RADIUS = 0.9
SHIFT = 0.5
DEPTH = 48
KRYLOV = 3
LANES = 128
f32 = jnp.float32
bf16 = jnp.bfloat16


def whole(memory):
    return pl.BlockSpec(memory_space=memory)


def split3(x):
    first = x.astype(bf16).astype(f32)
    rest = x - first
    second = rest.astype(bf16).astype(f32)
    return first, second, rest - second


def augmented(points, is_node):
    count = points.shape[1]
    row = lax.broadcasted_iota(jnp.int32, (8, count), 0)
    square = jnp.sum(points * points, axis=0, keepdims=True)
    one = jnp.ones_like(square)
    if is_node:
        coords, low, high = points, square, one
    else:
        coords, low, high = -2.0 * points, one, square
    zeros = jnp.zeros((5, count), f32)
    padded = jnp.concatenate([coords, zeros], axis=0)
    return jnp.where(row == 3, low, jnp.where(row == 4, high, padded))


def node_kernel(steps, centres_ref, nodes_ref, out_ref):
    step = pl.program_id(0)
    origin = centres_ref[:, 0:1]

    def fill(points):
        a, b, c = split3(augmented((points - origin) * (1.0 / RADIUS), True))
        rows = jnp.concatenate([a, b, a, b, c, a], axis=0)
        for t in range(out_ref.shape[0]):
            out_ref[t] = jnp.transpose(rows[:, t * BLK : (t + 1) * BLK]).astype(bf16)

    @pl.when(step < steps - 1)
    def _():
        fill(nodes_ref[...])

    @pl.when(step == steps - 1)
    def _():
        fill(centres_ref[...])


def prepare_nodes(centres, nodes):
    width = centres.shape[1]
    per_step = width // BLK
    node_steps = nodes.shape[1] // width
    steps = node_steps + 1
    return pl.pallas_call(
        functools.partial(node_kernel, steps),
        grid=(steps,),
        in_specs=[
            pl.BlockSpec((3, width), lambda i: (0, 0)),
            pl.BlockSpec((3, width), lambda i: (0, jnp.minimum(i, node_steps - 1))),
        ],
        out_specs=pl.BlockSpec((per_step, BLK, DEPTH), lambda i: (i, 0, 0)),
        out_shape=jax.ShapeDtypeStruct((steps * per_step, BLK, DEPTH), bf16),
        name="prepare_nodes",
    )(centres, nodes)


def centre_kernel(before_ref, own_ref, after_ref, out_ref):
    per = own_ref.shape[1] // BLK
    origin = own_ref[:, 0:1]
    for k, ref in enumerate((before_ref, own_ref, after_ref)):
        points = (ref[0:3, :] - origin[0:3]) * (1.0 / RADIUS)
        a, b, c = split3(augmented(points, False))
        rows = jnp.concatenate([a, a, b, b, a, c], axis=0)
        for t in range(per):
            out_ref[k * per + t] = rows[:, t * BLK : (t + 1) * BLK].astype(bf16)


def prepare_centres(before, own, after):
    per = own.shape[1] // BLK
    return pl.pallas_call(
        centre_kernel,
        in_specs=[whole(pltpu.VMEM)] * 3,
        out_specs=whole(pltpu.VMEM),
        out_shape=jax.ShapeDtypeStruct((3 * per, DEPTH, BLK), bf16),
        name="prepare_centres",
    )(before, own, after)


def phi(square):
    bounded = jnp.maximum(square, 1e-12)
    scaled = bounded * lax.rsqrt(bounded)
    remain = jnp.maximum(1.0 - scaled, 0.0)
    squared = remain * remain
    return (squared * squared * (scaled + 0.25)).astype(bf16)


def accumulate(
    unroll, together, tiles, group_count, places, members, left_ref, right_ref, weight_ref, total
):
    def clear(t, carry):
        total[t] = jnp.zeros((BLK, LANES), f32)
        return carry

    lax.fori_loop(0, tiles + 1, clear, 0)

    def step(g, carry):
        for h in range(unroll):
            group = g * unroll + h
            place = places[group]
            ids = [members[group * together + j] for j in range(together)]
            left = jnp.concatenate([left_ref[jnp.minimum(t, tiles - 1)] for t in ids], axis=0)
            square = jnp.dot(left, right_ref[place], preferred_element_type=f32)
            image = jnp.dot(phi(square), weight_ref[place], preferred_element_type=f32)
            for j, t in enumerate(ids):
                total[t] += image[j * BLK : (j + 1) * BLK]
        return carry

    lax.fori_loop(0, group_count, step, 0)


def fill_weights(weight_ref, fields, per):
    width = 2 * MODES * len(fields[0])
    for k, refs in enumerate(fields):
        stack = jnp.concatenate([r[...].astype(f32) for r in refs], axis=0) * 4.0
        high = stack.astype(bf16).astype(f32)
        low = stack - high
        rows = jnp.concatenate(
            [high, low, jnp.zeros((LANES - width, stack.shape[1]), f32)], axis=0
        )
        for t in range(per):
            weight_ref[k * per + t] = jnp.transpose(rows[:, t * BLK : (t + 1) * BLK]).astype(bf16)


def operator_kernel(
    unroll, together, tiles, count_ref, place_ref, member_ref, left_ref, right_ref,
    before_ref, own_ref, after_ref, out_ref, weight_ref, total,
):
    fill_weights(weight_ref, ((before_ref,), (own_ref,), (after_ref,)), tiles)
    accumulate(
        unroll, together, tiles, count_ref[0], place_ref, member_ref, left_ref, right_ref,
        weight_ref, total,
    )
    for t in range(tiles):
        image = jnp.transpose(total[t])
        sl = slice(t * BLK, (t + 1) * BLK)
        out_ref[:, sl] = image[0:MODES] + image[MODES : 2 * MODES] + SHIFT * own_ref[:, sl]


def apply_operator(unroll, together, lists, left, right, before, own, after):
    tiles = own.shape[1] // BLK
    last = left.shape[0] // tiles - 1
    vmem, smem = whole(pltpu.VMEM), whole(pltpu.SMEM)
    return pl.pallas_call(
        functools.partial(operator_kernel, unroll, together, tiles),
        grid=(1,),
        in_specs=[smem] * 3
        + [pl.BlockSpec((tiles, BLK, DEPTH), lambda i: (last, 0, 0))]
        + [vmem] * 4,
        out_specs=vmem,
        out_shape=jax.ShapeDtypeStruct(own.shape, f32),
        scratch_shapes=[
            pltpu.VMEM((3 * tiles, BLK, LANES), bf16),
            pltpu.VMEM((tiles + 1, BLK, LANES), f32),
        ],
        compiler_params=pltpu.CompilerParams(vmem_limit_bytes=40 * 2**20),
        name="operator",
    )(*lists, left, right, before, own, after)


def row_of(columns):
    mode = lax.broadcasted_iota(jnp.int32, (MODES, BLK), 0)
    lane = lax.broadcasted_iota(jnp.int32, (MODES, BLK), 1)
    spread = jnp.zeros((MODES, BLK), f32)
    for q, column in enumerate(columns):
        spread = jnp.where(lane == q * MODES + mode, column, spread)
    return jnp.sum(spread, axis=0, keepdims=True)


def columns_of(row, count):
    mode = lax.broadcasted_iota(jnp.int32, (MODES, BLK), 0)
    lane = lax.broadcasted_iota(jnp.int32, (MODES, BLK), 1)
    return [
        jnp.sum(jnp.where(lane == q * MODES + mode, row, 0.0), axis=1, keepdims=True)
        for q in range(count)
    ]


PAIRS = ((0, 0), (0, 1), (1, 1), (1, 2), (2, 2), (0, 2))


def volume_kernel(
    unroll, together, tiles, own_tiles, share, count_ref, place_ref, member_ref, left_ref, right_ref,
    *refs,
):
    fields = (refs[0:3], refs[3:6], refs[6:9])
    out_ref, sums_ref, weight_ref, total = refs[9:]
    fill_weights(weight_ref, fields, own_tiles)
    accumulate(
        unroll, together, tiles, count_ref[0], place_ref, member_ref, left_ref, right_ref,
        weight_ref, total,
    )
    wide = KRYLOV * MODES

    def finish(g, gram):
        for h in range(4):
            t = g * 4 + h
            image = jnp.transpose(total[t])
            image = image[0:wide] + image[wide : 2 * wide]
            out_ref[:, pl.ds(pl.multiple_of(t * BLK, BLK), BLK)] = image
            parts = [image[k * MODES : (k + 1) * MODES] for k in range(KRYLOV)]
            gram = tuple(s + parts[i] * parts[j] for s, (i, j) in zip(gram, PAIRS))
        return gram

    node_tiles = tiles - own_tiles
    gram = lax.fori_loop(
        0, node_tiles // 4, finish, tuple(jnp.zeros((MODES, BLK), f32) for _ in PAIRS)
    )
    columns = [jnp.sum(s, axis=1, keepdims=True) for s in gram]
    own = [r[...] for r in fields[1]]
    moments = [own[0] * own[0], own[0] * own[1], own[1] * own[1], own[1] * own[2], own[2] * own[2]]
    columns += [share * jnp.sum(s, axis=1, keepdims=True) for s in moments]
    last = jnp.zeros((MODES, BLK), f32)
    for b in range(own_tiles):
        image = jnp.transpose(total[node_tiles + b])
        piece = own[2][:, b * BLK : (b + 1) * BLK]
        low = 2 * MODES
        image = image[low : low + MODES] + image[wide + low : wide + low + MODES]
        last = last + piece * (image + SHIFT * piece)
    columns.append(share * jnp.sum(last, axis=1, keepdims=True))
    sums_ref[...] = jnp.broadcast_to(row_of(columns), sums_ref.shape)


def volume_images(unroll, together, lists, left, right, fields, devices, share):
    own_tiles = fields[1][0].shape[1] // BLK
    tiles = left.shape[0]
    nodes = (tiles - own_tiles) * BLK
    vmem, smem = whole(pltpu.VMEM), whole(pltpu.SMEM)
    return pl.pallas_call(
        functools.partial(volume_kernel, unroll, together, tiles, own_tiles, share),
        in_specs=[smem] * 3 + [vmem] * 11,
        out_specs=(vmem, vmem),
        out_shape=(
            jax.ShapeDtypeStruct((KRYLOV * MODES, nodes), f32),
            jax.ShapeDtypeStruct((devices, BLK), f32),
        ),
        scratch_shapes=[
            pltpu.VMEM((3 * own_tiles, BLK, LANES), bf16),
            pltpu.VMEM((tiles + 1, BLK, LANES), f32),
        ],
        compiler_params=pltpu.CompilerParams(vmem_limit_bytes=58 * 2**20),
        name="volume",
    )(*lists, left, right, *[f for side in fields for f in side])


def coefficients(row, total_nodes):
    columns = columns_of(row, 2 * len(PAIRS))
    gram, mu = columns[:6], columns[6:]
    zero = jnp.zeros_like(mu[0])
    one = jnp.ones_like(mu[0])

    def pairing(a, b, extra):
        out = zero
        for i, x in enumerate(a):
            for j, y in enumerate(b):
                out = out + x * y * mu[i + j + extra]
        return out

    residual, direction = [one], [one]
    answer = [zero, zero, zero]
    norm = mu[0]
    for iteration in range(KRYLOV):
        size = norm / pairing(direction, direction, 1)
        for i, x in enumerate(direction):
            answer[i] = answer[i] + size * x
        if iteration + 1 < KRYLOV:
            grown = residual + [zero]
            for i, x in enumerate(direction):
                grown[i + 1] = grown[i + 1] - size * x
            residual = grown
            later = pairing(residual, residual, 0)
            ratio = later / norm
            longer = direction + [zero]
            direction = [r + ratio * d for r, d in zip(residual, longer)]
            norm = later
    power = zero
    for s, (i, j) in zip(gram, PAIRS):
        power = power + (1.0 if i == j else 2.0) * s * answer[i] * answer[j]
    scale = jnp.sqrt(jnp.maximum(power, 0.0) / total_nodes + 1e-06)
    return answer, [a / scale for a in answer]


def combine_kernel(total_nodes, sums_ref, v0_ref, v1_ref, v2_ref, image_ref, weights_ref, out_ref, coef):
    @pl.when(pl.program_id(0) == 0)
    def _():
        row = jnp.sum(sums_ref[...], axis=0, keepdims=True)
        answer, scaled = coefficients(row, total_nodes)
        weights_ref[...] = answer[0] * v0_ref[...] + answer[1] * v1_ref[...] + answer[2] * v2_ref[...]
        for k, column in enumerate(scaled):
            coef[k] = jnp.broadcast_to(column, (MODES, LANES))

    c = [coef[k][:, 0:1] for k in range(KRYLOV)]
    out_ref[...] = (
        c[0] * image_ref[0:MODES]
        + c[1] * image_ref[MODES : 2 * MODES]
        + c[2] * image_ref[2 * MODES : 3 * MODES]
    )


def combine(sums, vectors, images, total_nodes):
    nodes = images.shape[1]
    width = 8192 if nodes % 8192 == 0 else nodes
    fixed = lambda i: (0, 0)
    moving = lambda i: (0, i)
    small = pl.BlockSpec(vectors[0].shape, fixed)
    return pl.pallas_call(
        functools.partial(combine_kernel, total_nodes),
        grid=(nodes // width,),
        in_specs=[pl.BlockSpec(sums.shape, fixed), small, small, small]
        + [pl.BlockSpec((KRYLOV * MODES, width), moving)],
        out_specs=(small, pl.BlockSpec((MODES, width), moving)),
        out_shape=(
            jax.ShapeDtypeStruct(vectors[0].shape, f32),
            jax.ShapeDtypeStruct((MODES, nodes), f32),
        ),
        scratch_shapes=[pltpu.VMEM((KRYLOV, MODES, LANES), f32)],
        name="combine",
    )(sums, *vectors, images)


def work_list(places, together, unroll, kinds):
    rows, slots = places.shape
    limit = -(-(rows * slots + kinds * (together - 1)) // together)
    limit = -(-limit // unroll) * unroll
    kind = jnp.arange(kinds, dtype=jnp.int32)
    present = jnp.any(places[:, :, None] == kind, axis=1).astype(f32)
    lower = (jnp.arange(rows)[:, None] >= jnp.arange(rows)[None, :]).astype(f32)
    reach = jnp.dot(lower, present, preferred_element_type=f32)
    groups = jnp.ceil(reach[-1] / together)
    before = (jnp.arange(kinds)[:, None] < jnp.arange(kinds)[None, :]).astype(f32)
    start = jnp.sum(before * groups[:, None], axis=0)
    end = start + groups
    index = jnp.arange(limit, dtype=jnp.int32).astype(f32)
    chosen = (index[:, None] >= start[None, :]) & (index[:, None] < end[None, :])
    place = jnp.sum(jnp.where(chosen, kind[None, :], 0), axis=1)
    first = together * (index - jnp.sum(jnp.where(chosen, start[None, :], 0.0), axis=1))
    reached = jnp.dot(chosen.astype(f32), reach.T, preferred_element_type=f32)
    rank = first[:, None] + jnp.arange(together).astype(f32)[None, :]
    member = jnp.sum((reached[:, None, :] <= rank[:, :, None]).astype(jnp.int32), axis=2)
    count = jnp.ceil(jnp.sum(groups) / unroll).astype(jnp.int32).reshape(1)
    return count, place.astype(jnp.int32), member.reshape(-1)


def halves(shard, axis):
    count = lax.axis_size(axis)
    up = [(i, i + 1) for i in range(count - 1)]
    down = [(i + 1, i) for i in range(count - 1)]
    return lax.ppermute(shard, axis, up), lax.ppermute(shard, axis, down)


def per_device(centres, mode_shapes, neighbours, volume_nodes, supports):
    blk_dev = neighbours.shape[0]
    kinds = 3 * blk_dev
    offset = (lax.axis_index("surf") - 1) * blk_dev
    devices = lax.axis_size("surf") * lax.axis_size("vol")
    share = 1.0 / lax.axis_size("vol")
    total_nodes = volume_nodes.shape[1] * devices

    packed = jnp.concatenate([centres, jnp.zeros((5, centres.shape[1]), f32), mode_shapes], axis=0)
    before, after = halves(packed, "surf")

    def place_of(ids):
        return jnp.where(ids >= 0, jnp.clip(ids - offset, 0, kinds - 1), -1)

    own_places = place_of(neighbours)
    left = prepare_nodes(centres, volume_nodes)
    own_list = work_list(own_places, 3, 4, kinds)
    whole_list = work_list(jnp.concatenate([place_of(supports), own_places]), 4, 4, kinds)

    right = prepare_centres(before, packed, after)
    v0 = mode_shapes
    v0_before, v0_after = before[8:], after[8:]
    v1 = apply_operator(4, 3, own_list, left, right, v0_before, v0, v0_after)
    v1_before, v1_after = halves(v1, "surf")
    v2 = apply_operator(4, 3, own_list, left, right, v1_before, v1, v1_after)
    v2_before, v2_after = halves(v2, "surf")
    fields = (
        (v0_before, v1_before, v2_before),
        (v0, v1, v2),
        (v0_after, v1_after, v2_after),
    )
    images, sums = volume_images(4, 4, whole_list, left, right, fields, devices, share)
    sums = lax.all_to_all(sums, ("surf", "vol"), 0, 0, tiled=True)
    return combine(sums, (v0, v1, v2), images, total_nodes)


def solution(mesh):
    return jax.shard_map(
        per_device,
        mesh=mesh,
        in_specs=(
            P(None, "surf"),
            P(None, "surf"),
            P("surf", None),
            P(None, ("surf", "vol")),
            P(("surf", "vol"), None),
        ),
        out_specs=(P(None, "surf"), P(None, ("surf", "vol"))),
        check_vma=False,
    )
```

```python
import functools

import jax
import jax.numpy as jnp
from jax import lax
from jax.experimental import pallas as pl
from jax.experimental.pallas import tpu as pltpu
from jax.sharding import PartitionSpec as P

MODES = 16
BLK = 256
RADIUS = 0.9
SHIFT = 0.5
DEPTH = 48
KRYLOV = 3
LANES = 128
f32 = jnp.float32
bf16 = jnp.bfloat16


def whole(memory):
    return pl.BlockSpec(memory_space=memory)


def split3(x):
    first = x.astype(bf16).astype(f32)
    rest = x - first
    second = rest.astype(bf16).astype(f32)
    return first, second, rest - second


def augmented(points, is_node):
    count = points.shape[1]
    row = lax.broadcasted_iota(jnp.int32, (8, count), 0)
    square = jnp.sum(points * points, axis=0, keepdims=True)
    one = jnp.ones_like(square)
    if is_node:
        coords, low, high = points, square, one
    else:
        coords, low, high = -2.0 * points, one, square
    zeros = jnp.zeros((5, count), f32)
    padded = jnp.concatenate([coords, zeros], axis=0)
    return jnp.where(row == 3, low, jnp.where(row == 4, high, padded))


def node_kernel(centres_ref, nodes_ref, out_ref):
    points = (nodes_ref[...] - centres_ref[:, 0:1]) * (1.0 / RADIUS)
    a, b, c = split3(augmented(points, True))
    rows = jnp.concatenate([a, b, a, b, c, a], axis=0)
    for t in range(out_ref.shape[0]):
        out_ref[t] = rows[:, t * BLK : (t + 1) * BLK].astype(bf16)


def prepare_nodes(centres, nodes):
    tiles = nodes.shape[1] // BLK
    step = 32 if tiles % 32 == 0 else tiles
    return pl.pallas_call(
        node_kernel,
        grid=(tiles // step,),
        in_specs=[
            pl.BlockSpec((3, BLK), lambda i: (0, 0)),
            pl.BlockSpec((3, step * BLK), lambda i: (0, i)),
        ],
        out_specs=pl.BlockSpec((step, DEPTH, BLK), lambda i: (i, 0, 0)),
        out_shape=jax.ShapeDtypeStruct((tiles, DEPTH, BLK), bf16),
        name="prepare_nodes",
    )(centres, nodes)


def centre_kernel(before_ref, own_ref, after_ref, out_ref):
    per = own_ref.shape[1] // BLK
    origin = own_ref[:, 0:1]
    for k, ref in enumerate((before_ref, own_ref, after_ref)):
        points = (ref[0:3, :] - origin[0:3]) * (1.0 / RADIUS)
        a, b, c = split3(augmented(points, False))
        rows = jnp.concatenate([a, a, b, b, a, c], axis=0)
        for t in range(per):
            out_ref[k * per + t] = rows[:, t * BLK : (t + 1) * BLK].astype(bf16)


def prepare_centres(before, own, after):
    per = own.shape[1] // BLK
    return pl.pallas_call(
        centre_kernel,
        in_specs=[whole(pltpu.VMEM)] * 3,
        out_specs=whole(pltpu.VMEM),
        out_shape=jax.ShapeDtypeStruct((3 * per, DEPTH, BLK), bf16),
        name="prepare_centres",
    )(before, own, after)


def pl_reciprocal(x):
    return pltpu.reciprocal(x, approx=True)


def phi(square):
    scaled = pl_reciprocal(lax.rsqrt(jnp.maximum(square, 1e-12)))
    remain = jnp.maximum(1.0 - scaled, 0.0)
    squared = remain * remain
    return (squared * squared * (scaled + 0.25)).astype(bf16)


def clear(tiles, total):
    def one(t, carry):
        total[t] = jnp.zeros((BLK, LANES), f32)
        return carry

    lax.fori_loop(0, tiles + 1, one, 0)


def accumulate(
    unroll, together, tiles, group_count, places, members, left_ref, right_ref, weight_ref, total
):
    def step(g, carry):
        for h in range(unroll):
            group = g * unroll + h
            place = places[group]
            ids = [members[group * together + j] for j in range(together)]
            left = jnp.concatenate([left_ref[jnp.minimum(t, tiles - 1)] for t in ids], axis=1)
            square = lax.dot_general(
                left, right_ref[place], (((0,), (0,)), ((), ())), preferred_element_type=f32
            )
            image = jnp.dot(phi(square), weight_ref[place], preferred_element_type=f32)
            for j, t in enumerate(ids):
                total[t] += image[j * BLK : (j + 1) * BLK]
        return carry

    lax.fori_loop(0, group_count, step, 0)


def fill_weights(weight_ref, fields, per):
    width = 2 * MODES * len(fields[0])
    for k, refs in enumerate(fields):
        stack = jnp.concatenate([r[...].astype(f32) for r in refs], axis=0) * 4.0
        high = stack.astype(bf16).astype(f32)
        low = stack - high
        rows = jnp.concatenate(
            [high, low, jnp.zeros((LANES - width, stack.shape[1]), f32)], axis=0
        )
        for t in range(per):
            weight_ref[k * per + t] = jnp.transpose(rows[:, t * BLK : (t + 1) * BLK]).astype(bf16)


def operator_kernel(
    unroll, together, tiles, count_ref, place_ref, member_ref, left_ref, right_ref,
    before_ref, own_ref, after_ref, out_ref, weight_ref, total,
):
    fill_weights(weight_ref, ((before_ref,), (own_ref,), (after_ref,)), tiles)
    clear(tiles, total)
    accumulate(
        unroll, together, tiles, count_ref[0], place_ref, member_ref, left_ref, right_ref,
        weight_ref, total,
    )
    for t in range(tiles):
        image = jnp.transpose(total[t])
        sl = slice(t * BLK, (t + 1) * BLK)
        out_ref[:, sl] = image[0:MODES] + image[MODES : 2 * MODES] + SHIFT * own_ref[:, sl]


def apply_operator(unroll, together, lists, left, right, before, own, after):
    tiles = own.shape[1] // BLK
    vmem, smem = whole(pltpu.VMEM), whole(pltpu.SMEM)
    return pl.pallas_call(
        functools.partial(operator_kernel, unroll, together, tiles),
        in_specs=[smem] * 3 + [vmem] * 5,
        out_specs=vmem,
        out_shape=jax.ShapeDtypeStruct(own.shape, f32),
        scratch_shapes=[
            pltpu.VMEM((3 * tiles, BLK, LANES), bf16),
            pltpu.VMEM((tiles + 1, BLK, LANES), f32),
        ],
        compiler_params=pltpu.CompilerParams(vmem_limit_bytes=40 * 2**20),
        name="operator",
    )(*lists, left, right, before, own, after)


def row_of(columns):
    mode = lax.broadcasted_iota(jnp.int32, (MODES, BLK), 0)
    lane = lax.broadcasted_iota(jnp.int32, (MODES, BLK), 1)
    spread = jnp.zeros((MODES, BLK), f32)
    for q, column in enumerate(columns):
        spread = jnp.where(lane == q * MODES + mode, column, spread)
    return jnp.sum(spread, axis=0, keepdims=True)


def columns_of(row, count):
    mode = lax.broadcasted_iota(jnp.int32, (MODES, BLK), 0)
    lane = lax.broadcasted_iota(jnp.int32, (MODES, BLK), 1)
    return [
        jnp.sum(jnp.where(lane == q * MODES + mode, row, 0.0), axis=1, keepdims=True)
        for q in range(count)
    ]


PAIRS = ((0, 0), (0, 1), (1, 1), (1, 2), (2, 2), (0, 2))


def volume_kernel(
    unroll, together, sizes, share, count_ref, place_ref, member_ref, turn_ref, right_ref, *refs
):
    lefts, fields = refs[0:3], (refs[3:6], refs[6:9], refs[9:12])
    out_ref, guest_ref, sums_ref, weight_ref, total, left_ref, image_ref, sems, sent = refs[12:]
    own, guests, checks = sizes
    tiles = own + guests + checks
    turn = turn_ref[0]
    spans = (
        (lefts[0], left_ref.at[pl.ds(0, own)]),
        (lefts[1], left_ref.at[pl.ds(own, guests)]),
        (lefts[2].at[pl.ds(turn * checks, checks)], left_ref.at[pl.ds(own + guests, checks)]),
    )
    copies = [pltpu.make_async_copy(a, b, sems.at[i]) for i, (a, b) in enumerate(spans)]
    for copy in copies:
        copy.start()
    per = fields[1][0].shape[1] // BLK
    fill_weights(weight_ref, fields, per)
    clear(tiles, total)
    for copy in copies:
        copy.wait()
    accumulate(
        unroll, together, tiles, count_ref[0], place_ref, member_ref, left_ref, right_ref,
        weight_ref, total,
    )
    wide = KRYLOV * MODES
    zeros = tuple(jnp.zeros((MODES, BLK), f32) for _ in PAIRS)

    def finish(first, ref, sem, steps, g, gram):
        for h in range(steps):
            t = first + g * steps + h
            image = jnp.transpose(total[t])
            image = image[0:wide] + image[wide : 2 * wide]
            image_ref[:, pl.ds(pl.multiple_of(t * BLK, BLK), BLK)] = image
            parts = [image[k * MODES : (k + 1) * MODES] for k in range(KRYLOV)]
            gram = tuple(s + parts[i] * parts[j] for s, (i, j) in zip(gram, PAIRS))
        width = steps * BLK
        start = pl.multiple_of(first * BLK + g * width, BLK)
        pltpu.make_async_copy(
            image_ref.at[:, pl.ds(start, width)],
            ref.at[:, pl.ds(pl.multiple_of(g * width, BLK), width)],
            sem,
        ).start()
        return gram

    def steps_of(count):
        return next(n for n in (4, 5, 3, 2, 1) if count % n == 0)

    n = steps_of(guests)
    gram = lax.fori_loop(0, guests // n, functools.partial(finish, own, guest_ref, sent.at[1], n), zeros)
    n = steps_of(own)
    gram = lax.fori_loop(0, own // n, functools.partial(finish, 0, out_ref, sent.at[0], n), gram)
    columns = [jnp.sum(s, axis=1, keepdims=True) for s in gram]
    v = [r[...] for r in fields[1]]
    moments = [v[0] * v[0], v[0] * v[1], v[1] * v[1], v[1] * v[2], v[2] * v[2]]
    columns += [share * jnp.sum(s, axis=1, keepdims=True) for s in moments]
    last = jnp.zeros((MODES, BLK), f32)
    low = 2 * MODES
    for b in range(checks):
        image = jnp.transpose(total[own + guests + b])
        start = pl.multiple_of((turn * checks + b) * BLK, BLK)
        piece = fields[1][2][:, pl.ds(start, BLK)]
        image = image[low : low + MODES] + image[wide + low : wide + low + MODES]
        last = last + piece * (image + SHIFT * piece)
    columns.append(jnp.sum(last, axis=1, keepdims=True))
    row = row_of(columns)
    pair = jnp.concatenate([row[:, 0:LANES], row[:, LANES : 2 * LANES]], axis=0)
    sums_ref[...] = jnp.broadcast_to(pair[None], sums_ref.shape)
    pltpu.make_async_copy(image_ref.at[:, pl.ds(0, own * BLK)], out_ref, sent.at[0]).wait()
    pltpu.make_async_copy(image_ref.at[:, pl.ds(own * BLK, guests * BLK)], guest_ref, sent.at[1]).wait()


def volume_images(unroll, together, lists, turn, right, lefts, checks, fields, devices, share):
    per = fields[1][0].shape[1] // BLK
    own, guests = lefts[0].shape[0], lefts[1].shape[0]
    tiles = own + guests + checks
    vmem, smem, far = whole(pltpu.VMEM), whole(pltpu.SMEM), whole(pl.ANY)
    return pl.pallas_call(
        functools.partial(volume_kernel, unroll, together, (own, guests, checks), share),
        in_specs=[smem] * 4 + [vmem] + [far] * 3 + [vmem] * 9,
        out_specs=(far, far, vmem),
        out_shape=(
            jax.ShapeDtypeStruct((KRYLOV * MODES, own * BLK), f32),
            jax.ShapeDtypeStruct((KRYLOV * MODES, guests * BLK), f32),
            jax.ShapeDtypeStruct((devices, 2, LANES), f32),
        ),
        scratch_shapes=[
            pltpu.VMEM((3 * per, BLK, LANES), bf16),
            pltpu.VMEM((tiles + 1, BLK, LANES), f32),
            pltpu.VMEM((tiles, DEPTH, BLK), bf16),
            pltpu.VMEM((KRYLOV * MODES, (own + guests) * BLK), f32),
            pltpu.SemaphoreType.DMA((3,)),
            pltpu.SemaphoreType.DMA((2,)),
        ],
        compiler_params=pltpu.CompilerParams(vmem_limit_bytes=58 * 2**20),
        name="volume",
    )(*lists, turn, right, *lefts, *[f for side in fields for f in side])


def coefficients(row, total_nodes):
    columns = columns_of(row, 2 * len(PAIRS))
    gram, mu = columns[:6], columns[6:]
    zero = jnp.zeros_like(mu[0])
    one = jnp.ones_like(mu[0])

    def pairing(a, b, extra):
        out = zero
        for i, x in enumerate(a):
            for j, y in enumerate(b):
                out = out + x * y * mu[i + j + extra]
        return out

    residual, direction = [one], [one]
    answer = [zero, zero, zero]
    norm = mu[0]
    for iteration in range(KRYLOV):
        size = norm / pairing(direction, direction, 1)
        for i, x in enumerate(direction):
            answer[i] = answer[i] + size * x
        if iteration + 1 < KRYLOV:
            grown = residual + [zero]
            for i, x in enumerate(direction):
                grown[i + 1] = grown[i + 1] - size * x
            residual = grown
            later = pairing(residual, residual, 0)
            ratio = later / norm
            longer = direction + [zero]
            direction = [r + ratio * d for r, d in zip(residual, longer)]
            norm = later
    power = zero
    for s, (i, j) in zip(gram, PAIRS):
        power = power + (1.0 if i == j else 2.0) * s * answer[i] * answer[j]
    scale = jnp.sqrt(jnp.maximum(power, 0.0) / total_nodes + 1e-06)
    return answer, [a / scale for a in answer]


def settle_kernel(total_nodes, sums_ref, v0_ref, v1_ref, v2_ref, guest_ref, weights_ref, coef_ref, out_ref):
    pair = jnp.sum(sums_ref[...], axis=0)
    row = jnp.concatenate([pair[0:1], pair[1:2]], axis=1)
    answer, scaled = coefficients(row, total_nodes)
    weights_ref[...] = answer[0] * v0_ref[...] + answer[1] * v1_ref[...] + answer[2] * v2_ref[...]
    for k, column in enumerate(scaled):
        coef_ref[k] = jnp.broadcast_to(column, (MODES, LANES))
    out_ref[...] = blend(scaled, guest_ref).astype(bf16)


def blend(c, image_ref):
    return (
        c[0] * image_ref[0:MODES]
        + c[1] * image_ref[MODES : 2 * MODES]
        + c[2] * image_ref[2 * MODES : 3 * MODES]
    )


def settle(sums, vectors, guests, total_nodes):
    vmem = whole(pltpu.VMEM)
    return pl.pallas_call(
        functools.partial(settle_kernel, total_nodes),
        in_specs=[vmem] * 5,
        out_specs=(vmem,) * 3,
        out_shape=(
            jax.ShapeDtypeStruct(vectors[0].shape, f32),
            jax.ShapeDtypeStruct((KRYLOV, MODES, LANES), f32),
            jax.ShapeDtypeStruct((MODES, guests.shape[1]), bf16),
        ),
        name="settle",
    )(sums, *vectors, guests)


def combine_kernel(coef_ref, image_ref, out_ref):
    out_ref[...] = blend([coef_ref[k][:, 0:1] for k in range(KRYLOV)], image_ref)


def combine(coef, images):
    nodes = images.shape[1]
    width = 8192 if nodes % 8192 == 0 else nodes
    return pl.pallas_call(
        combine_kernel,
        grid=(nodes // width,),
        in_specs=[
            pl.BlockSpec(coef.shape, lambda i: (0, 0, 0)),
            pl.BlockSpec((KRYLOV * MODES, width), lambda i: (0, i)),
        ],
        out_specs=pl.BlockSpec((MODES, width), lambda i: (0, i)),
        out_shape=jax.ShapeDtypeStruct((MODES, nodes), f32),
        name="combine",
    )(coef, images)


def insert_kernel(kept, turn_ref, *refs):
    parts, out_ref, wide, sems = refs[1:-3], refs[-3], refs[-2], refs[-1]

    @pl.when(turn_ref[0] == 0)
    def _():
        width = parts[0].shape[1]
        copies = []
        for k, part in enumerate(parts):
            wide[k] = part[...].astype(f32)
            target = out_ref.at[:, pl.ds((kept + k * width // BLK) * BLK, width)]
            copy = pltpu.make_async_copy(wide.at[k], target, sems.at[k])
            copy.start()
            copies.append(copy)
        for copy in copies:
            copy.wait()


def insert(turn, main, parts, kept):
    vmem, far = whole(pltpu.VMEM), whole(pl.ANY)
    return pl.pallas_call(
        functools.partial(insert_kernel, kept),
        in_specs=[whole(pltpu.SMEM), far] + [vmem] * len(parts),
        out_specs=far,
        out_shape=jax.ShapeDtypeStruct(main.shape, f32),
        input_output_aliases={1: 0},
        scratch_shapes=[
            pltpu.VMEM((len(parts),) + parts[0].shape, f32),
            pltpu.SemaphoreType.DMA((len(parts),)),
        ],
        name="insert",
    )(turn, main, *parts)


def work_list(places, together, unroll, kinds):
    rows, slots = places.shape
    limit = -(-(rows * slots + kinds * (together - 1)) // together)
    limit = -(-limit // unroll) * unroll
    kind = jnp.arange(kinds, dtype=jnp.int32)
    present = jnp.any(places[:, :, None] == kind, axis=1).astype(f32)
    lower = (jnp.arange(rows)[:, None] >= jnp.arange(rows)[None, :]).astype(f32)
    reach = jnp.dot(lower, present, preferred_element_type=f32)
    groups = jnp.ceil(reach[-1] / together)
    before = (jnp.arange(kinds)[:, None] < jnp.arange(kinds)[None, :]).astype(f32)
    start = jnp.sum(before * groups[:, None], axis=0)
    end = start + groups
    index = jnp.arange(limit, dtype=jnp.int32).astype(f32)
    chosen = (index[:, None] >= start[None, :]) & (index[:, None] < end[None, :])
    place = jnp.sum(jnp.where(chosen, kind[None, :], 0), axis=1)
    first = together * (index - jnp.sum(jnp.where(chosen, start[None, :], 0.0), axis=1))
    reached = jnp.dot(chosen.astype(f32), reach.T, preferred_element_type=f32)
    rank = first[:, None] + jnp.arange(together).astype(f32)[None, :]
    member = jnp.sum((reached[:, None, :] <= rank[:, :, None]).astype(jnp.int32), axis=2)
    count = jnp.ceil(jnp.sum(groups) / unroll).astype(jnp.int32).reshape(1)
    return count, place.astype(jnp.int32), member.reshape(-1)


def neighbour_pairs(axis):
    count = lax.axis_size(axis)
    return [(i, i + 1) for i in range(count - 1)], [(i + 1, i) for i in range(count - 1)]


MOVED_SHARE = 20 / 128


def helper_turns(count):
    return (1, 2, count - 2) if count >= 6 else (1,)


def per_device(centres, mode_shapes, neighbours, volume_nodes, supports):
    blk_dev = neighbours.shape[0]
    tile_dev, slots = supports.shape
    kinds = 3 * blk_dev
    offset = (lax.axis_index("surf") - 1) * blk_dev
    helpers = helper_turns(lax.axis_size("vol"))
    turn = lax.axis_index("vol")
    turns = turn.astype(jnp.int32).reshape(1)
    devices = lax.axis_size("surf") * lax.axis_size("vol")
    share = 1.0 / lax.axis_size("vol")
    checks = blk_dev // lax.axis_size("vol")
    total_nodes = volume_nodes.shape[1] * devices
    moved = int(tile_dev * MOVED_SHARE)
    kept = tile_dev - len(helpers) * moved

    packed = jnp.concatenate([centres, jnp.zeros((5, centres.shape[1]), f32), mode_shapes], axis=0)
    up, down = neighbour_pairs("surf")
    before = lax.ppermute(packed, "surf", up)

    def place_of(ids):
        return jnp.where(ids >= 0, jnp.clip(ids - offset, 0, kinds - 1), -1)

    own_places = place_of(neighbours)
    own_list = work_list(own_places, 3, 4, kinds)
    own_left = prepare_nodes(centres, centres)
    again, own_left = lax.optimization_barrier((packed, own_left))
    after = lax.ppermute(again, "surf", down)
    left = prepare_nodes(centres, volume_nodes)

    right = prepare_centres(before, packed, after)
    ids = jnp.pad(supports[kept:].astype(f32), ((0, 0), (0, BLK - slots))).reshape(1, -1)
    parcel = jnp.concatenate([volume_nodes[:, kept * BLK :], ids], axis=0)
    parcel, right = lax.optimization_barrier((parcel, right))
    width = moved * BLK
    got = jnp.zeros((4, width), f32)
    helping = False
    for k, helper in enumerate(helpers):
        piece = parcel[:, k * width : (k + 1) * width]
        got = got + lax.ppermute(piece, "vol", [(0, helper)])
        helping = helping | (turn == helper)
    guest_ids = got[3].reshape(moved, BLK)[:, :slots].astype(jnp.int32)
    guest_places = jnp.where(helping, place_of(guest_ids), -1)
    kept_here = (turn > 0) | (jnp.arange(tile_dev) < kept)
    tile_places = jnp.where(kept_here[:, None], place_of(supports), -1)
    check_places = lax.dynamic_slice_in_dim(own_places, turn * checks, checks, axis=0)
    places = jnp.concatenate([tile_places, guest_places, check_places], axis=0)
    whole_list = work_list(places, 4, 4, kinds)
    guest_left = prepare_nodes(centres, got[:3])

    v0 = mode_shapes
    v0_before, v0_after = before[8:], after[8:]
    v1 = apply_operator(4, 3, own_list, own_left, right, v0_before, v0, v0_after)
    v1_before, v1_after = lax.ppermute(v1, "surf", up), lax.ppermute(v1, "surf", down)
    v2 = apply_operator(4, 3, own_list, own_left, right, v1_before, v1, v1_after)
    v2_before, v2_after = lax.ppermute(v2, "surf", up), lax.ppermute(v2, "surf", down)
    fields = (
        (v0_before, v1_before, v2_before),
        (v0, v1, v2),
        (v0_after, v1_after, v2_after),
    )
    lefts = (left, guest_left, own_left)
    images, guests, sums = volume_images(
        4, 4, whole_list, turns, right, lefts, checks, fields, devices, share
    )
    sums = lax.all_to_all(sums, ("surf", "vol"), 0, 0, tiled=True)
    weights, coef, away = settle(sums, (v0, v1, v2), guests, total_nodes)
    parts = [lax.ppermute(away, "vol", [(helper, 0)]) for helper in helpers]
    return weights, insert(turns, combine(coef, images), parts, kept)


def solution(mesh):
    return jax.shard_map(
        per_device,
        mesh=mesh,
        in_specs=(
            P(None, "surf"),
            P(None, "surf"),
            P("surf", None),
            P(None, ("surf", "vol")),
            P(("surf", "vol"), None),
        ),
        out_specs=(P(None, "surf"), P(None, ("surf", "vol"))),
        check_vma=False,
    )
```

```python
import functools

import jax
import jax.numpy as jnp
from jax import lax
from jax.experimental import pallas as pl
from jax.experimental.pallas import tpu as pltpu
from jax.sharding import PartitionSpec as P

MODES = 16
BLK = 256
RADIUS = 0.9
SHIFT = 0.5
DEPTH = 48
KRYLOV = 3
LANES = 128
f32 = jnp.float32
bf16 = jnp.bfloat16


def whole(memory):
    return pl.BlockSpec(memory_space=memory)


def split3(x):
    first = x.astype(bf16).astype(f32)
    rest = x - first
    second = rest.astype(bf16).astype(f32)
    return first, second, rest - second


def augmented(points, is_node):
    count = points.shape[1]
    row = lax.broadcasted_iota(jnp.int32, (8, count), 0)
    square = jnp.sum(points * points, axis=0, keepdims=True)
    one = jnp.ones_like(square)
    if is_node:
        coords, low, high = points, square, one
    else:
        coords, low, high = -2.0 * points, one, square
    zeros = jnp.zeros((5, count), f32)
    padded = jnp.concatenate([coords, zeros], axis=0)
    return jnp.where(row == 3, low, jnp.where(row == 4, high, padded))


def node_kernel(centres_ref, nodes_ref, out_ref):
    points = (nodes_ref[...] - centres_ref[:, 0:1]) * (1.0 / RADIUS)
    a, b, c = split3(augmented(points, True))
    rows = jnp.concatenate([a, b, a, b, c, a], axis=0)
    for t in range(out_ref.shape[0]):
        out_ref[t] = rows[:, t * BLK : (t + 1) * BLK].astype(bf16)


def prepare_nodes(centres, nodes):
    tiles = nodes.shape[1] // BLK
    step = 32 if tiles % 32 == 0 else tiles
    return pl.pallas_call(
        node_kernel,
        grid=(tiles // step,),
        in_specs=[
            pl.BlockSpec((3, BLK), lambda i: (0, 0)),
            pl.BlockSpec((3, step * BLK), lambda i: (0, i)),
        ],
        out_specs=pl.BlockSpec((step, DEPTH, BLK), lambda i: (i, 0, 0)),
        out_shape=jax.ShapeDtypeStruct((tiles, DEPTH, BLK), bf16),
        name="prepare_nodes",
    )(centres, nodes)


def centre_kernel(before_ref, own_ref, after_ref, out_ref):
    per = own_ref.shape[1] // BLK
    origin = own_ref[:, 0:1]
    for k, ref in enumerate((before_ref, own_ref, after_ref)):
        points = (ref[0:3, :] - origin[0:3]) * (1.0 / RADIUS)
        a, b, c = split3(augmented(points, False))
        rows = jnp.concatenate([a, a, b, b, a, c], axis=0)
        for t in range(per):
            out_ref[k * per + t] = rows[:, t * BLK : (t + 1) * BLK].astype(bf16)


def prepare_centres(before, own, after):
    per = own.shape[1] // BLK
    return pl.pallas_call(
        centre_kernel,
        in_specs=[whole(pltpu.VMEM)] * 3,
        out_specs=whole(pltpu.VMEM),
        out_shape=jax.ShapeDtypeStruct((3 * per, DEPTH, BLK), bf16),
        name="prepare_centres",
    )(before, own, after)


def pl_reciprocal(x):
    return pltpu.reciprocal(x, approx=True)


def phi(square):
    scaled = pl_reciprocal(lax.rsqrt(jnp.maximum(square, 1e-12)))
    remain = jnp.maximum(1.0 - scaled, 0.0)
    squared = remain * remain
    return (squared * squared * (scaled + 0.25)).astype(bf16)


def clear(tiles, total):
    def one(t, carry):
        total[t] = jnp.zeros((BLK, LANES), f32)
        return carry

    lax.fori_loop(0, tiles + 1, one, 0)


def accumulate(
    unroll, together, tiles, group_count, places, members, left_ref, right_ref, weight_ref, total
):
    def step(g, carry):
        for h in range(unroll):
            group = g * unroll + h
            place = places[group]
            ids = [members[group * together + j] for j in range(together)]
            left = jnp.concatenate([left_ref[jnp.minimum(t, tiles - 1)] for t in ids], axis=1)
            square = lax.dot_general(
                left, right_ref[place], (((0,), (0,)), ((), ())), preferred_element_type=f32
            )
            image = jnp.dot(phi(square), weight_ref[place], preferred_element_type=f32)
            for j, t in enumerate(ids):
                total[t] += image[j * BLK : (j + 1) * BLK]
        return carry

    lax.fori_loop(0, group_count, step, 0)


def modes_of(ref):
    return ref[ref.shape[0] - MODES :, :]


def fill_weights(weight_ref, fields, per):
    width = 2 * MODES * len(fields[0])
    for k, refs in enumerate(fields):
        stack = jnp.concatenate([modes_of(r).astype(f32) for r in refs], axis=0) * 4.0
        high = stack.astype(bf16).astype(f32)
        low = stack - high
        rows = jnp.concatenate(
            [high, low, jnp.zeros((LANES - width, stack.shape[1]), f32)], axis=0
        )
        for t in range(per):
            weight_ref[k * per + t] = jnp.transpose(rows[:, t * BLK : (t + 1) * BLK]).astype(bf16)


def operator_kernel(
    unroll, together, tiles, count_ref, place_ref, member_ref, left_ref, right_ref,
    before_ref, own_ref, after_ref, out_ref, weight_ref, total,
):
    fill_weights(weight_ref, ((before_ref,), (own_ref,), (after_ref,)), tiles)
    clear(tiles, total)
    accumulate(
        unroll, together, tiles, count_ref[0], place_ref, member_ref, left_ref, right_ref,
        weight_ref, total,
    )
    for t in range(tiles):
        image = jnp.transpose(total[t])
        sl = slice(t * BLK, (t + 1) * BLK)
        out_ref[:, sl] = image[0:MODES] + image[MODES : 2 * MODES] + SHIFT * own_ref[:, sl]


def apply_operator(unroll, together, lists, left, right, before, own, after):
    tiles = own.shape[1] // BLK
    vmem, smem = whole(pltpu.VMEM), whole(pltpu.SMEM)
    return pl.pallas_call(
        functools.partial(operator_kernel, unroll, together, tiles),
        in_specs=[smem] * 3 + [vmem] * 5,
        out_specs=vmem,
        out_shape=jax.ShapeDtypeStruct(own.shape, f32),
        scratch_shapes=[
            pltpu.VMEM((3 * tiles, BLK, LANES), bf16),
            pltpu.VMEM((tiles + 1, BLK, LANES), f32),
        ],
        compiler_params=pltpu.CompilerParams(vmem_limit_bytes=40 * 2**20),
        name="operator",
    )(*lists, left, right, before, own, after)


def row_of(columns):
    mode = lax.broadcasted_iota(jnp.int32, (MODES, BLK), 0)
    lane = lax.broadcasted_iota(jnp.int32, (MODES, BLK), 1)
    spread = jnp.zeros((MODES, BLK), f32)
    for q, column in enumerate(columns):
        spread = jnp.where(lane == q * MODES + mode, column, spread)
    return jnp.sum(spread, axis=0, keepdims=True)


def columns_of(row, count):
    mode = lax.broadcasted_iota(jnp.int32, (MODES, BLK), 0)
    lane = lax.broadcasted_iota(jnp.int32, (MODES, BLK), 1)
    return [
        jnp.sum(jnp.where(lane == q * MODES + mode, row, 0.0), axis=1, keepdims=True)
        for q in range(count)
    ]


PAIRS = ((0, 0), (0, 1), (1, 1), (1, 2), (2, 2), (0, 2))


def volume_kernel(
    unroll, together, sizes, share, count_ref, place_ref, member_ref, turn_ref, right_ref, *refs
):
    lefts, fields = refs[0:3], (refs[3:6], refs[6:9], refs[9:12])
    out_ref, guest_ref, sums_ref, weight_ref, total, left_ref, image_ref, sems, sent = refs[12:]
    own, guests, checks = sizes
    tiles = own + guests + checks
    turn = turn_ref[0]
    spans = (
        (lefts[0], left_ref.at[pl.ds(0, own)]),
        (lefts[1], left_ref.at[pl.ds(own, guests)]),
        (lefts[2].at[pl.ds(turn * checks, checks)], left_ref.at[pl.ds(own + guests, checks)]),
    )
    copies = [pltpu.make_async_copy(a, b, sems.at[i]) for i, (a, b) in enumerate(spans)]
    for copy in copies:
        copy.start()
    per = fields[1][0].shape[1] // BLK
    fill_weights(weight_ref, fields, per)
    clear(tiles, total)
    for copy in copies:
        copy.wait()
    accumulate(
        unroll, together, tiles, count_ref[0], place_ref, member_ref, left_ref, right_ref,
        weight_ref, total,
    )
    wide = KRYLOV * MODES
    zeros = tuple(jnp.zeros((MODES, BLK), f32) for _ in PAIRS)

    def finish(first, ref, sem, steps, g, gram):
        for h in range(steps):
            t = first + g * steps + h
            image = jnp.transpose(total[t])
            image = image[0:wide] + image[wide : 2 * wide]
            image_ref[:, pl.ds(pl.multiple_of(t * BLK, BLK), BLK)] = image
            parts = [image[k * MODES : (k + 1) * MODES] for k in range(KRYLOV)]
            gram = tuple(s + parts[i] * parts[j] for s, (i, j) in zip(gram, PAIRS))
        width = steps * BLK
        start = pl.multiple_of(first * BLK + g * width, BLK)
        pltpu.make_async_copy(
            image_ref.at[:, pl.ds(start, width)],
            ref.at[:, pl.ds(pl.multiple_of(g * width, BLK), width)],
            sem,
        ).start()
        return gram

    def steps_of(count):
        return next(n for n in (8, 4, 5, 3, 2, 1) if count % n == 0)

    n = steps_of(guests)
    gram = lax.fori_loop(0, guests // n, functools.partial(finish, own, guest_ref, sent.at[1], n), zeros)
    n = steps_of(own)
    gram = lax.fori_loop(0, own // n, functools.partial(finish, 0, out_ref, sent.at[0], n), gram)
    columns = [jnp.sum(s, axis=1, keepdims=True) for s in gram]
    v = [r[...] for r in fields[1]]
    moments = [v[0] * v[0], v[0] * v[1], v[1] * v[1], v[1] * v[2], v[2] * v[2]]
    columns += [share * jnp.sum(s, axis=1, keepdims=True) for s in moments]
    last = jnp.zeros((MODES, BLK), f32)
    low = 2 * MODES
    for b in range(checks):
        image = jnp.transpose(total[own + guests + b])
        start = pl.multiple_of((turn * checks + b) * BLK, BLK)
        piece = fields[1][2][:, pl.ds(start, BLK)]
        image = image[low : low + MODES] + image[wide + low : wide + low + MODES]
        last = last + piece * (image + SHIFT * piece)
    columns.append(jnp.sum(last, axis=1, keepdims=True))
    row = row_of(columns)
    pair = jnp.concatenate([row[:, 0:LANES], row[:, LANES : 2 * LANES]], axis=0)
    sums_ref[...] = jnp.broadcast_to(pair[None], sums_ref.shape)
    pltpu.make_async_copy(image_ref.at[:, pl.ds(0, own * BLK)], out_ref, sent.at[0]).wait()
    pltpu.make_async_copy(image_ref.at[:, pl.ds(own * BLK, guests * BLK)], guest_ref, sent.at[1]).wait()


def volume_images(unroll, together, lists, turn, right, lefts, checks, fields, devices, share):
    per = fields[1][0].shape[1] // BLK
    own, guests = lefts[0].shape[0], lefts[1].shape[0]
    tiles = own + guests + checks
    vmem, smem, far = whole(pltpu.VMEM), whole(pltpu.SMEM), whole(pl.ANY)
    return pl.pallas_call(
        functools.partial(volume_kernel, unroll, together, (own, guests, checks), share),
        in_specs=[smem] * 4 + [vmem] + [far] * 3 + [vmem] * 9,
        out_specs=(far, far, vmem),
        out_shape=(
            jax.ShapeDtypeStruct((KRYLOV * MODES, own * BLK), f32),
            jax.ShapeDtypeStruct((KRYLOV * MODES, guests * BLK), f32),
            jax.ShapeDtypeStruct((devices, 2, LANES), f32),
        ),
        scratch_shapes=[
            pltpu.VMEM((3 * per, BLK, LANES), bf16),
            pltpu.VMEM((tiles + 1, BLK, LANES), f32),
            pltpu.VMEM((tiles, DEPTH, BLK), bf16),
            pltpu.VMEM((KRYLOV * MODES, (own + guests) * BLK), f32),
            pltpu.SemaphoreType.DMA((3,)),
            pltpu.SemaphoreType.DMA((2,)),
        ],
        compiler_params=pltpu.CompilerParams(vmem_limit_bytes=58 * 2**20),
        name="volume",
    )(*lists, turn, right, *lefts, *[f for side in fields for f in side])


def coefficients(row, total_nodes):
    columns = columns_of(row, 2 * len(PAIRS))
    gram, mu = columns[:6], columns[6:]
    zero = jnp.zeros_like(mu[0])
    one = jnp.ones_like(mu[0])

    def pairing(a, b, extra):
        out = zero
        for i, x in enumerate(a):
            for j, y in enumerate(b):
                out = out + x * y * mu[i + j + extra]
        return out

    residual, direction = [one], [one]
    answer = [zero, zero, zero]
    norm = mu[0]
    for iteration in range(KRYLOV):
        size = norm / pairing(direction, direction, 1)
        for i, x in enumerate(direction):
            answer[i] = answer[i] + size * x
        if iteration + 1 < KRYLOV:
            grown = residual + [zero]
            for i, x in enumerate(direction):
                grown[i + 1] = grown[i + 1] - size * x
            residual = grown
            later = pairing(residual, residual, 0)
            ratio = later / norm
            longer = direction + [zero]
            direction = [r + ratio * d for r, d in zip(residual, longer)]
            norm = later
    power = zero
    for s, (i, j) in zip(gram, PAIRS):
        power = power + (1.0 if i == j else 2.0) * s * answer[i] * answer[j]
    scale = jnp.sqrt(jnp.maximum(power, 0.0) / total_nodes + 1e-06)
    return answer, [a / scale for a in answer]


def settle_kernel(total_nodes, sums_ref, v0_ref, v1_ref, v2_ref, guest_ref, weights_ref, coef_ref, out_ref):
    pair = jnp.sum(sums_ref[...], axis=0)
    row = jnp.concatenate([pair[0:1], pair[1:2]], axis=1)
    answer, scaled = coefficients(row, total_nodes)
    weights_ref[...] = answer[0] * v0_ref[...] + answer[1] * v1_ref[...] + answer[2] * v2_ref[...]
    for k, column in enumerate(scaled):
        coef_ref[k] = jnp.broadcast_to(column, (MODES, LANES))
    out_ref[...] = blend(scaled, guest_ref).astype(bf16)


def blend(c, image_ref):
    return (
        c[0] * image_ref[0:MODES]
        + c[1] * image_ref[MODES : 2 * MODES]
        + c[2] * image_ref[2 * MODES : 3 * MODES]
    )


def settle(sums, vectors, guests, total_nodes):
    vmem = whole(pltpu.VMEM)
    return pl.pallas_call(
        functools.partial(settle_kernel, total_nodes),
        in_specs=[vmem] * 5,
        out_specs=(vmem,) * 3,
        out_shape=(
            jax.ShapeDtypeStruct(vectors[0].shape, f32),
            jax.ShapeDtypeStruct((KRYLOV, MODES, LANES), f32),
            jax.ShapeDtypeStruct((MODES, guests.shape[1]), bf16),
        ),
        name="settle",
    )(sums, *vectors, guests)


def combine_kernel(coef_ref, image_ref, out_ref):
    out_ref[...] = blend([coef_ref[k][:, 0:1] for k in range(KRYLOV)], image_ref)


def combine(coef, images):
    nodes = images.shape[1]
    width = 8192 if nodes % 8192 == 0 else nodes
    return pl.pallas_call(
        combine_kernel,
        grid=(nodes // width,),
        in_specs=[
            pl.BlockSpec(coef.shape, lambda i: (0, 0, 0)),
            pl.BlockSpec((KRYLOV * MODES, width), lambda i: (0, i)),
        ],
        out_specs=pl.BlockSpec((MODES, width), lambda i: (0, i)),
        out_shape=jax.ShapeDtypeStruct((MODES, nodes), f32),
        name="combine",
    )(coef, images)


def insert_kernel(kept, turn_ref, *refs):
    parts, out_ref, wide, sems = refs[1:-3], refs[-3], refs[-2], refs[-1]

    @pl.when(turn_ref[0] == 0)
    def _():
        width = parts[0].shape[1]
        copies = []
        for k, part in enumerate(parts):
            wide[k] = part[...].astype(f32)
            target = out_ref.at[:, pl.ds((kept + k * width // BLK) * BLK, width)]
            copy = pltpu.make_async_copy(wide.at[k], target, sems.at[k])
            copy.start()
            copies.append(copy)
        for copy in copies:
            copy.wait()


def insert(turn, main, parts, kept):
    vmem, far = whole(pltpu.VMEM), whole(pl.ANY)
    return pl.pallas_call(
        functools.partial(insert_kernel, kept),
        in_specs=[whole(pltpu.SMEM), far] + [vmem] * len(parts),
        out_specs=far,
        out_shape=jax.ShapeDtypeStruct(main.shape, f32),
        input_output_aliases={1: 0},
        scratch_shapes=[
            pltpu.VMEM((len(parts),) + parts[0].shape, f32),
            pltpu.SemaphoreType.DMA((len(parts),)),
        ],
        name="insert",
    )(turn, main, *parts)


def work_list(places, together, unroll, kinds):
    rows, slots = places.shape
    limit = -(-(rows * slots + kinds * (together - 1)) // together)
    limit = -(-limit // unroll) * unroll
    kind = jnp.arange(kinds, dtype=jnp.int32)
    present = jnp.any(places[:, :, None] == kind, axis=1).astype(f32)
    lower = (jnp.arange(rows)[:, None] >= jnp.arange(rows)[None, :]).astype(f32)
    reach = jnp.dot(lower, present, preferred_element_type=f32)
    groups = jnp.ceil(reach[-1] / together)
    before = (jnp.arange(kinds)[:, None] < jnp.arange(kinds)[None, :]).astype(f32)
    start = jnp.sum(before * groups[:, None], axis=0)
    end = start + groups
    index = jnp.arange(limit, dtype=jnp.int32).astype(f32)
    chosen = (index[:, None] >= start[None, :]) & (index[:, None] < end[None, :])
    place = jnp.sum(jnp.where(chosen, kind[None, :], 0), axis=1)
    first = together * (index - jnp.sum(jnp.where(chosen, start[None, :], 0.0), axis=1))
    reached = jnp.dot(chosen.astype(f32), reach.T, preferred_element_type=f32)
    rank = first[:, None] + jnp.arange(together).astype(f32)[None, :]
    member = jnp.sum((reached[:, None, :] <= rank[:, :, None]).astype(jnp.int32), axis=2)
    count = jnp.ceil(jnp.sum(groups) / unroll).astype(jnp.int32).reshape(1)
    return count, place.astype(jnp.int32), member.reshape(-1)


def neighbour_pairs(axis):
    count = lax.axis_size(axis)
    return [(i, i + 1) for i in range(count - 1)], [(i + 1, i) for i in range(count - 1)]


MOVED_SHARE = 1 / 8


def helper_turns(count):
    return (1, 2, count - 2, count - 1) if count >= 6 else (1,)


def per_device(centres, mode_shapes, neighbours, volume_nodes, supports):
    blk_dev = neighbours.shape[0]
    tile_dev, slots = supports.shape
    kinds = 3 * blk_dev
    offset = (lax.axis_index("surf") - 1) * blk_dev
    helpers = helper_turns(lax.axis_size("vol"))
    turn = lax.axis_index("vol")
    turns = turn.astype(jnp.int32).reshape(1)
    devices = lax.axis_size("surf") * lax.axis_size("vol")
    share = 1.0 / lax.axis_size("vol")
    checks = blk_dev // lax.axis_size("vol")
    total_nodes = volume_nodes.shape[1] * devices
    moved = int(tile_dev * MOVED_SHARE)
    kept = tile_dev - len(helpers) * moved

    packed = jnp.concatenate([centres, jnp.zeros((5, centres.shape[1]), f32), mode_shapes], axis=0)
    up, down = neighbour_pairs("surf")
    before = lax.ppermute(packed, "surf", up)

    def place_of(ids):
        return jnp.where(ids >= 0, jnp.clip(ids - offset, 0, kinds - 1), -1)

    own_places = place_of(neighbours)
    own_list = work_list(own_places, 3, 8, kinds)
    own_left = prepare_nodes(centres, centres)
    again, own_left = lax.optimization_barrier((packed, own_left))
    after = lax.ppermute(again, "surf", down)
    left = prepare_nodes(centres, volume_nodes)

    right = prepare_centres(before, packed, after)
    v0 = mode_shapes
    v1 = apply_operator(8, 3, own_list, own_left, right, before, v0, after)
    v1_low = v1.astype(bf16)
    v1_before = lax.ppermute(v1_low, "surf", up)
    v1_after = lax.ppermute(v1_low, "surf", down)

    ids = jnp.pad(supports[kept:].astype(f32), ((0, 0), (0, BLK - slots))).reshape(1, -1)
    parcel = jnp.concatenate([volume_nodes[:, kept * BLK :], ids], axis=0)
    parcel, v1_before = lax.optimization_barrier((parcel, v1_before))
    width = moved * BLK
    got = jnp.zeros((4, width), f32)
    helping = False
    for k, helper in enumerate(helpers):
        piece = parcel[:, k * width : (k + 1) * width]
        got = got + lax.ppermute(piece, "vol", [(0, helper)])
        helping = helping | (turn == helper)
    guest_ids = got[3].reshape(moved, BLK)[:, :slots].astype(jnp.int32)
    guest_places = jnp.where(helping, place_of(guest_ids), -1)
    kept_here = (turn > 0) | (jnp.arange(tile_dev) < kept)
    tile_places = jnp.where(kept_here[:, None], place_of(supports), -1)
    check_places = lax.dynamic_slice_in_dim(own_places, turn * checks, checks, axis=0)
    places = jnp.concatenate([tile_places, guest_places, check_places], axis=0)
    whole_list = work_list(places, 2, 10, kinds)
    guest_left = prepare_nodes(centres, got[:3])

    v2 = apply_operator(8, 3, own_list, own_left, right, v1_before, v1, v1_after)
    v2_low = v2.astype(bf16)
    v2_before = lax.ppermute(v2_low, "surf", up)
    v2_after = lax.ppermute(v2_low, "surf", down)
    fields = (
        (before, v1_before, v2_before),
        (v0, v1, v2),
        (after, v1_after, v2_after),
    )
    lefts = (left, guest_left, own_left)
    images, guests, sums = volume_images(
        10, 2, whole_list, turns, right, lefts, checks, fields, devices, share
    )
    sums = lax.all_to_all(sums, ("surf", "vol"), 0, 0, tiled=True)
    weights, coef, away = settle(sums, (v0, v1, v2), guests, total_nodes)
    parts = [lax.ppermute(away, "vol", [(helper, 0)]) for helper in helpers]
    return weights, insert(turns, combine(coef, images), parts, kept)


def solution(mesh):
    return jax.shard_map(
        per_device,
        mesh=mesh,
        in_specs=(
            P(None, "surf"),
            P(None, "surf"),
            P("surf", None),
            P(None, ("surf", "vol")),
            P(("surf", "vol"), None),
        ),
        out_specs=(P(None, "surf"), P(None, ("surf", "vol"))),
        check_vma=False,
    )
```

```python
import functools

import jax
import jax.numpy as jnp
from jax import lax
from jax.experimental import pallas as pl
from jax.experimental.pallas import tpu as pltpu
from jax.sharding import PartitionSpec as P

MODES = 16
BLK = 256
RADIUS = 0.9
SHIFT = 0.5
DEPTH = 48
KRYLOV = 3
LANES = 128
f32 = jnp.float32
bf16 = jnp.bfloat16


def whole(memory):
    return pl.BlockSpec(memory_space=memory)


def split3(x):
    first = x.astype(bf16).astype(f32)
    rest = x - first
    second = rest.astype(bf16).astype(f32)
    return first, second, rest - second


def augmented(points, is_node):
    count = points.shape[1]
    row = lax.broadcasted_iota(jnp.int32, (8, count), 0)
    square = jnp.sum(points * points, axis=0, keepdims=True)
    one = jnp.ones_like(square)
    if is_node:
        coords, low, high = points, square, one
    else:
        coords, low, high = -2.0 * points, one, square
    zeros = jnp.zeros((5, count), f32)
    padded = jnp.concatenate([coords, zeros], axis=0)
    return jnp.where(row == 3, low, jnp.where(row == 4, high, padded))


def node_kernel(centres_ref, nodes_ref, out_ref):
    points = (nodes_ref[...] - centres_ref[:, 0:1]) * (1.0 / RADIUS)
    a, b, c = split3(augmented(points, True))
    rows = jnp.concatenate([a, b, a, b, c, a], axis=0)
    for t in range(out_ref.shape[0]):
        out_ref[t] = rows[:, t * BLK : (t + 1) * BLK].astype(bf16)


def prepare_nodes(centres, nodes):
    tiles = nodes.shape[1] // BLK
    step = 32 if tiles % 32 == 0 else tiles
    return pl.pallas_call(
        node_kernel,
        grid=(tiles // step,),
        in_specs=[
            pl.BlockSpec((3, BLK), lambda i: (0, 0)),
            pl.BlockSpec((3, step * BLK), lambda i: (0, i)),
        ],
        out_specs=pl.BlockSpec((step, DEPTH, BLK), lambda i: (i, 0, 0)),
        out_shape=jax.ShapeDtypeStruct((tiles, DEPTH, BLK), bf16),
        name="prepare_nodes",
    )(centres, nodes)


def fill_centres(out_ref, before_ref, own_ref, after_ref):
    per = own_ref.shape[1] // BLK
    origin = own_ref[0:3, 0:1]
    for k, ref in enumerate((before_ref, own_ref, after_ref)):
        points = (ref[0:3, :] - origin) * (1.0 / RADIUS)
        a, b, c = split3(augmented(points, False))
        rows = jnp.concatenate([a, a, b, b, a, c], axis=0)
        for t in range(per):
            out_ref[k * per + t] = rows[:, t * BLK : (t + 1) * BLK].astype(bf16)


def pl_reciprocal(x):
    return pltpu.reciprocal(x, approx=True)


def phi(square):
    scaled = pl_reciprocal(lax.rsqrt(jnp.maximum(square, 1e-12)))
    remain = jnp.maximum(1.0 - scaled, 0.0)
    squared = remain * remain
    return (squared * squared * (scaled + 0.25)).astype(bf16)


def clear(tiles, total):
    def one(t, carry):
        total[t] = jnp.zeros((BLK, LANES), f32)
        return carry

    lax.fori_loop(0, tiles + 1, one, 0)


def accumulate(
    unroll, together, tiles, group_count, places, members, left_ref, right_ref, weight_ref, total
):
    def step(g, carry):
        for h in range(unroll):
            group = g * unroll + h
            place = places[group]
            ids = [members[group * together + j] for j in range(together)]
            left = jnp.concatenate([left_ref[jnp.minimum(t, tiles - 1)] for t in ids], axis=1)
            square = lax.dot_general(
                left, right_ref[place], (((0,), (0,)), ((), ())), preferred_element_type=f32
            )
            image = jnp.dot(phi(square), weight_ref[place], preferred_element_type=f32)
            for j, t in enumerate(ids):
                total[t] += image[j * BLK : (j + 1) * BLK]
        return carry

    lax.fori_loop(0, group_count, step, 0)


def modes_of(ref):
    return ref[ref.shape[0] - MODES :, :]


def fill_weights(weight_ref, fields, per):
    width = 2 * MODES * len(fields[0])
    for k, refs in enumerate(fields):
        stack = jnp.concatenate([modes_of(r).astype(f32) for r in refs], axis=0) * 4.0
        high = stack.astype(bf16).astype(f32)
        low = stack - high
        rows = jnp.concatenate(
            [high, low, jnp.zeros((LANES - width, stack.shape[1]), f32)], axis=0
        )
        for t in range(per):
            weight_ref[k * per + t] = jnp.transpose(rows[:, t * BLK : (t + 1) * BLK]).astype(bf16)


def operator_kernel(unroll, together, tiles, first, count_ref, place_ref, member_ref, left_ref, *refs):
    if first:
        before_ref, own_ref, after_ref, out_ref, right_ref, weight_ref, total = refs
        fill_centres(right_ref, before_ref, own_ref, after_ref)
    else:
        right_ref, before_ref, own_ref, after_ref, out_ref, weight_ref, total = refs
    fill_weights(weight_ref, ((before_ref,), (own_ref,), (after_ref,)), tiles)
    clear(tiles, total)
    accumulate(
        unroll, together, tiles, count_ref[0], place_ref, member_ref, left_ref, right_ref,
        weight_ref, total,
    )
    own = modes_of(own_ref)
    for t in range(tiles):
        image = jnp.transpose(total[t])
        sl = slice(t * BLK, (t + 1) * BLK)
        out_ref[:, sl] = image[0:MODES] + image[MODES : 2 * MODES] + SHIFT * own[:, sl]


def apply_operator(unroll, together, lists, left, right, before, own, after):
    tiles = own.shape[1] // BLK
    vmem, smem = whole(pltpu.VMEM), whole(pltpu.SMEM)
    first = right is None
    image = jax.ShapeDtypeStruct((MODES, own.shape[1]), f32)
    factors = jax.ShapeDtypeStruct((3 * tiles, DEPTH, BLK), bf16)
    return pl.pallas_call(
        functools.partial(operator_kernel, unroll, together, tiles, first),
        in_specs=[smem] * 3 + [vmem] * (4 if first else 5),
        out_specs=(vmem, vmem) if first else vmem,
        out_shape=(image, factors) if first else image,
        scratch_shapes=[
            pltpu.VMEM((3 * tiles, BLK, LANES), bf16),
            pltpu.VMEM((tiles + 1, BLK, LANES), f32),
        ],
        compiler_params=pltpu.CompilerParams(vmem_limit_bytes=40 * 2**20),
        name="operator",
    )(*lists, left, *(() if first else (right,)), before, own, after)


def row_of(columns):
    mode = lax.broadcasted_iota(jnp.int32, (MODES, BLK), 0)
    lane = lax.broadcasted_iota(jnp.int32, (MODES, BLK), 1)
    spread = jnp.zeros((MODES, BLK), f32)
    for q, column in enumerate(columns):
        spread = jnp.where(lane == q * MODES + mode, column, spread)
    return jnp.sum(spread, axis=0, keepdims=True)


def columns_of(row, count):
    mode = lax.broadcasted_iota(jnp.int32, (MODES, BLK), 0)
    lane = lax.broadcasted_iota(jnp.int32, (MODES, BLK), 1)
    return [
        jnp.sum(jnp.where(lane == q * MODES + mode, row, 0.0), axis=1, keepdims=True)
        for q in range(count)
    ]


PAIRS = ((0, 0), (0, 1), (1, 1), (1, 2), (2, 2), (0, 2))


def volume_kernel(
    unroll, together, sizes, share, count_ref, place_ref, member_ref, turn_ref, right_ref, *refs
):
    lefts, fields = refs[0:3], (refs[3:6], refs[6:9], refs[9:12])
    out_ref, guest_ref, sums_ref, weight_ref, total, left_ref, image_ref, sems, sent = refs[12:]
    own, guests, checks = sizes
    tiles = own + guests + checks
    turn = turn_ref[0]
    spans = (
        (lefts[0], left_ref.at[pl.ds(0, own)]),
        (lefts[1], left_ref.at[pl.ds(own, guests)]),
        (lefts[2].at[pl.ds(turn * checks, checks)], left_ref.at[pl.ds(own + guests, checks)]),
    )
    copies = [pltpu.make_async_copy(a, b, sems.at[i]) for i, (a, b) in enumerate(spans)]
    for copy in copies:
        copy.start()
    per = fields[1][0].shape[1] // BLK
    fill_weights(weight_ref, fields, per)
    clear(tiles, total)
    for copy in copies:
        copy.wait()
    accumulate(
        unroll, together, tiles, count_ref[0], place_ref, member_ref, left_ref, right_ref,
        weight_ref, total,
    )
    wide = KRYLOV * MODES
    zeros = tuple(jnp.zeros((MODES, BLK), f32) for _ in PAIRS)

    def finish(first, ref, sem, steps, g, gram):
        for h in range(steps):
            t = first + g * steps + h
            image = jnp.transpose(total[t])
            image = image[0:wide] + image[wide : 2 * wide]
            image_ref[:, pl.ds(pl.multiple_of(t * BLK, BLK), BLK)] = image
            parts = [image[k * MODES : (k + 1) * MODES] for k in range(KRYLOV)]
            gram = tuple(s + parts[i] * parts[j] for s, (i, j) in zip(gram, PAIRS))
        width = steps * BLK
        start = pl.multiple_of(first * BLK + g * width, BLK)
        pltpu.make_async_copy(
            image_ref.at[:, pl.ds(start, width)],
            ref.at[:, pl.ds(pl.multiple_of(g * width, BLK), width)],
            sem,
        ).start()
        return gram

    def steps_of(count):
        return next(n for n in (8, 4, 5, 3, 2, 1) if count % n == 0)

    n = steps_of(guests)
    gram = lax.fori_loop(0, guests // n, functools.partial(finish, own, guest_ref, sent.at[1], n), zeros)
    n = steps_of(own)
    gram = lax.fori_loop(0, own // n, functools.partial(finish, 0, out_ref, sent.at[0], n), gram)
    columns = [jnp.sum(s, axis=1, keepdims=True) for s in gram]
    v = [r[...] for r in fields[1]]
    moments = [v[0] * v[0], v[0] * v[1], v[1] * v[1], v[1] * v[2], v[2] * v[2]]
    columns += [share * jnp.sum(s, axis=1, keepdims=True) for s in moments]
    last = jnp.zeros((MODES, BLK), f32)
    low = 2 * MODES
    for b in range(checks):
        image = jnp.transpose(total[own + guests + b])
        start = pl.multiple_of((turn * checks + b) * BLK, BLK)
        piece = fields[1][2][:, pl.ds(start, BLK)]
        image = image[low : low + MODES] + image[wide + low : wide + low + MODES]
        last = last + piece * (image + SHIFT * piece)
    columns.append(jnp.sum(last, axis=1, keepdims=True))
    row = row_of(columns)
    pair = jnp.concatenate([row[:, 0:LANES], row[:, LANES : 2 * LANES]], axis=0)
    sums_ref[...] = jnp.broadcast_to(pair[None], sums_ref.shape)
    pltpu.make_async_copy(image_ref.at[:, pl.ds(0, own * BLK)], out_ref, sent.at[0]).wait()
    pltpu.make_async_copy(image_ref.at[:, pl.ds(own * BLK, guests * BLK)], guest_ref, sent.at[1]).wait()


def volume_images(unroll, together, lists, turn, right, lefts, checks, fields, devices, share):
    per = fields[1][0].shape[1] // BLK
    own, guests = lefts[0].shape[0], lefts[1].shape[0]
    tiles = own + guests + checks
    vmem, smem, far = whole(pltpu.VMEM), whole(pltpu.SMEM), whole(pl.ANY)
    return pl.pallas_call(
        functools.partial(volume_kernel, unroll, together, (own, guests, checks), share),
        in_specs=[smem] * 4 + [vmem] + [far] * 3 + [vmem] * 9,
        out_specs=(far, far, vmem),
        out_shape=(
            jax.ShapeDtypeStruct((KRYLOV * MODES, own * BLK), f32),
            jax.ShapeDtypeStruct((KRYLOV * MODES, guests * BLK), f32),
            jax.ShapeDtypeStruct((devices, 2, LANES), f32),
        ),
        scratch_shapes=[
            pltpu.VMEM((3 * per, BLK, LANES), bf16),
            pltpu.VMEM((tiles + 1, BLK, LANES), f32),
            pltpu.VMEM((tiles, DEPTH, BLK), bf16),
            pltpu.VMEM((KRYLOV * MODES, (own + guests) * BLK), f32),
            pltpu.SemaphoreType.DMA((3,)),
            pltpu.SemaphoreType.DMA((2,)),
        ],
        compiler_params=pltpu.CompilerParams(vmem_limit_bytes=58 * 2**20),
        name="volume",
    )(*lists, turn, right, *lefts, *[f for side in fields for f in side])


def coefficients(row, total_nodes):
    columns = columns_of(row, 2 * len(PAIRS))
    gram, mu = columns[:6], columns[6:]
    zero = jnp.zeros_like(mu[0])
    one = jnp.ones_like(mu[0])

    def pairing(a, b, extra):
        out = zero
        for i, x in enumerate(a):
            for j, y in enumerate(b):
                out = out + x * y * mu[i + j + extra]
        return out

    residual, direction = [one], [one]
    answer = [zero, zero, zero]
    norm = mu[0]
    for iteration in range(KRYLOV):
        size = norm / pairing(direction, direction, 1)
        for i, x in enumerate(direction):
            answer[i] = answer[i] + size * x
        if iteration + 1 < KRYLOV:
            grown = residual + [zero]
            for i, x in enumerate(direction):
                grown[i + 1] = grown[i + 1] - size * x
            residual = grown
            later = pairing(residual, residual, 0)
            ratio = later / norm
            longer = direction + [zero]
            direction = [r + ratio * d for r, d in zip(residual, longer)]
            norm = later
    power = zero
    for s, (i, j) in zip(gram, PAIRS):
        power = power + (1.0 if i == j else 2.0) * s * answer[i] * answer[j]
    scale = jnp.sqrt(jnp.maximum(power, 0.0) / total_nodes + 1e-06)
    return answer, [a / scale for a in answer]


def settle_kernel(total_nodes, sums_ref, v0_ref, v1_ref, v2_ref, guest_ref, weights_ref, coef_ref, out_ref):
    pair = jnp.sum(sums_ref[...], axis=0)
    row = jnp.concatenate([pair[0:1], pair[1:2]], axis=1)
    answer, scaled = coefficients(row, total_nodes)
    weights_ref[...] = answer[0] * v0_ref[...] + answer[1] * v1_ref[...] + answer[2] * v2_ref[...]
    for k, column in enumerate(scaled):
        coef_ref[k] = jnp.broadcast_to(column, (MODES, LANES))
    out_ref[...] = blend(scaled, guest_ref).astype(bf16)


def blend(c, image_ref):
    return (
        c[0] * image_ref[0:MODES]
        + c[1] * image_ref[MODES : 2 * MODES]
        + c[2] * image_ref[2 * MODES : 3 * MODES]
    )


def settle(sums, vectors, guests, total_nodes):
    vmem = whole(pltpu.VMEM)
    return pl.pallas_call(
        functools.partial(settle_kernel, total_nodes),
        in_specs=[vmem] * 5,
        out_specs=(vmem,) * 3,
        out_shape=(
            jax.ShapeDtypeStruct(vectors[0].shape, f32),
            jax.ShapeDtypeStruct((KRYLOV, MODES, LANES), f32),
            jax.ShapeDtypeStruct((MODES, guests.shape[1]), bf16),
        ),
        name="settle",
    )(sums, *vectors, guests)


def combine_kernel(kept, turn_ref, coef_ref, image_ref, *refs):
    parts, out_ref = refs[:-1], refs[-1]
    step = pl.program_id(0)
    elsewhere = (turn_ref[0] == 0) & (step >= kept)

    @pl.when(jnp.logical_not(elsewhere))
    def _():
        out_ref[...] = blend([coef_ref[k][:, 0:1] for k in range(KRYLOV)], image_ref)

    for k, part in enumerate(parts):

        @pl.when(elsewhere & (step == kept + k))
        def _(part=part):
            out_ref[...] = part[...].astype(f32)


def combine(turn, coef, images, parts, kept):
    nodes = images.shape[1]
    width = parts[0].shape[1]
    return pl.pallas_call(
        functools.partial(combine_kernel, kept // width),
        grid=(nodes // width,),
        in_specs=[
            whole(pltpu.SMEM),
            pl.BlockSpec(coef.shape, lambda i: (0, 0, 0)),
            pl.BlockSpec((KRYLOV * MODES, width), lambda i: (0, i)),
        ]
        + [pl.BlockSpec(part.shape, lambda i: (0, 0)) for part in parts],
        out_specs=pl.BlockSpec((MODES, width), lambda i: (0, i)),
        out_shape=jax.ShapeDtypeStruct((MODES, nodes), f32),
        name="combine",
    )(turn, coef, images, *parts)


def work_list(places, together, unroll, kinds):
    rows, slots = places.shape
    limit = -(-(rows * slots + kinds * (together - 1)) // together)
    limit = -(-limit // unroll) * unroll
    kind = jnp.arange(kinds, dtype=jnp.int32)
    present = jnp.any(places[:, :, None] == kind, axis=1).astype(f32)
    lower = (jnp.arange(rows)[:, None] >= jnp.arange(rows)[None, :]).astype(f32)
    reach = jnp.dot(lower, present, preferred_element_type=f32)
    groups = jnp.ceil(reach[-1] / together)
    before = (jnp.arange(kinds)[:, None] < jnp.arange(kinds)[None, :]).astype(f32)
    start = jnp.sum(before * groups[:, None], axis=0)
    end = start + groups
    index = jnp.arange(limit, dtype=jnp.int32).astype(f32)
    chosen = (index[:, None] >= start[None, :]) & (index[:, None] < end[None, :])
    place = jnp.sum(jnp.where(chosen, kind[None, :], 0), axis=1)
    first = together * (index - jnp.sum(jnp.where(chosen, start[None, :], 0.0), axis=1))
    reached = jnp.dot(chosen.astype(f32), reach.T, preferred_element_type=f32)
    rank = first[:, None] + jnp.arange(together).astype(f32)[None, :]
    member = jnp.sum((reached[:, None, :] <= rank[:, :, None]).astype(jnp.int32), axis=2)
    count = jnp.ceil(jnp.sum(groups) / unroll).astype(jnp.int32).reshape(1)
    return count, place.astype(jnp.int32), member.reshape(-1)


def neighbour_pairs(axis):
    count = lax.axis_size(axis)
    return [(i, i + 1) for i in range(count - 1)], [(i + 1, i) for i in range(count - 1)]


MOVED_SHARE = 1 / 8


def helper_turns(count):
    return (1, 2, count - 2, count - 1) if count >= 6 else (1,)


def per_device(centres, mode_shapes, neighbours, volume_nodes, supports):
    blk_dev = neighbours.shape[0]
    tile_dev, slots = supports.shape
    kinds = 3 * blk_dev
    offset = (lax.axis_index("surf") - 1) * blk_dev
    helpers = helper_turns(lax.axis_size("vol"))
    turn = lax.axis_index("vol")
    turns = turn.astype(jnp.int32).reshape(1)
    devices = lax.axis_size("surf") * lax.axis_size("vol")
    share = 1.0 / lax.axis_size("vol")
    checks = blk_dev // lax.axis_size("vol")
    total_nodes = volume_nodes.shape[1] * devices
    moved = int(tile_dev * MOVED_SHARE)
    kept = tile_dev - len(helpers) * moved

    packed = jnp.concatenate([centres, jnp.zeros((5, centres.shape[1]), f32), mode_shapes], axis=0)
    up, down = neighbour_pairs("surf")
    before = lax.ppermute(packed, "surf", up)

    def place_of(ids):
        return jnp.where(ids >= 0, jnp.clip(ids - offset, 0, kinds - 1), -1)

    own_places = place_of(neighbours)
    own_list = work_list(own_places, 3, 8, kinds)
    own_left = prepare_nodes(centres, centres)
    again, own_left, own_list = lax.optimization_barrier((packed, own_left, own_list))
    after = lax.ppermute(again, "surf", down)

    v0 = mode_shapes
    v1, right = apply_operator(8, 3, own_list, own_left, None, before, packed, after)
    v1_low = v1.astype(bf16)
    v1_before = lax.ppermute(v1_low, "surf", up)
    later_nodes, again = lax.optimization_barrier((volume_nodes, v1_low))
    left = prepare_nodes(centres, later_nodes)
    again, left = lax.optimization_barrier((again, left))
    v1_after = lax.ppermute(again, "surf", down)

    ids = jnp.pad(supports[kept:].astype(f32), ((0, 0), (0, BLK - slots))).reshape(1, -1)
    parcel = jnp.concatenate([volume_nodes[:, kept * BLK :], ids], axis=0)
    parcel, v1_before = lax.optimization_barrier((parcel, v1_before))
    width = moved * BLK
    got = jnp.zeros((4, width), f32)
    helping = False
    for k, helper in enumerate(helpers):
        piece = parcel[:, k * width : (k + 1) * width]
        got = got + lax.ppermute(piece, "vol", [(0, helper)])
        helping = helping | (turn == helper)
    v2 = apply_operator(8, 3, own_list, own_left, right, v1_before, v1, v1_after)
    v2_low = v2.astype(bf16)
    v2_before = lax.ppermute(v2_low, "surf", up)
    got, again = lax.optimization_barrier((got, v2_low))
    guest_left = prepare_nodes(centres, got[:3])
    again, guest_left = lax.optimization_barrier((again, guest_left))
    v2_after = lax.ppermute(again, "surf", down)

    guest_ids = got[3].reshape(moved, BLK)[:, :slots].astype(jnp.int32)
    guest_places = jnp.where(helping, place_of(guest_ids), -1)
    kept_here = (turn > 0) | (jnp.arange(tile_dev) < kept)
    tile_places = jnp.where(kept_here[:, None], place_of(supports), -1)
    check_places = lax.dynamic_slice_in_dim(own_places, turn * checks, checks, axis=0)
    places = jnp.concatenate([tile_places, guest_places, check_places], axis=0)
    whole_list = work_list(places, 2, 10, kinds)
    fields = (
        (before, v1_before, v2_before),
        (v0, v1, v2),
        (after, v1_after, v2_after),
    )
    lefts = (left, guest_left, own_left)
    images, guests, sums = volume_images(
        10, 2, whole_list, turns, right, lefts, checks, fields, devices, share
    )
    sums = lax.all_to_all(sums, ("surf", "vol"), 0, 0, tiled=True)
    weights, coef, away = settle(sums, (v0, v1, v2), guests, total_nodes)
    parts = [lax.ppermute(away, "vol", [(helper, 0)]) for helper in helpers]
    return weights, combine(turns, coef, images, parts, kept * BLK)


def solution(mesh):
    return jax.shard_map(
        per_device,
        mesh=mesh,
        in_specs=(
            P(None, "surf"),
            P(None, "surf"),
            P("surf", None),
            P(None, ("surf", "vol")),
            P(("surf", "vol"), None),
        ),
        out_specs=(P(None, "surf"), P(None, ("surf", "vol"))),
        check_vma=False,
    )
```

```python
import functools

import jax
import jax.numpy as jnp
from jax import lax
from jax.experimental import pallas as pl
from jax.experimental.pallas import tpu as pltpu
from jax.sharding import PartitionSpec as P

MODES = 16
BLK = 256
RADIUS = 0.9
SHIFT = 0.5
DEPTH = 48
KRYLOV = 3
LANES = 128
f32 = jnp.float32
bf16 = jnp.bfloat16


def whole(memory):
    return pl.BlockSpec(memory_space=memory)


def split3(x):
    first = x.astype(bf16).astype(f32)
    rest = x - first
    second = rest.astype(bf16).astype(f32)
    return first, second, rest - second


def augmented(points, is_node):
    count = points.shape[1]
    row = lax.broadcasted_iota(jnp.int32, (8, count), 0)
    square = jnp.sum(points * points, axis=0, keepdims=True)
    one = jnp.ones_like(square)
    if is_node:
        coords, low, high = points, square, one
    else:
        coords, low, high = -2.0 * points, one, square
    zeros = jnp.zeros((5, count), f32)
    padded = jnp.concatenate([coords, zeros], axis=0)
    return jnp.where(row == 3, low, jnp.where(row == 4, high, padded))


def node_kernel(centres_ref, nodes_ref, out_ref):
    points = (nodes_ref[...] - centres_ref[:, 0:1]) * (1.0 / RADIUS)
    a, b, c = split3(augmented(points, True))
    rows = jnp.concatenate([a, b, a, b, c, a], axis=0)
    for t in range(out_ref.shape[0]):
        out_ref[t] = rows[:, t * BLK : (t + 1) * BLK].astype(bf16)


def prepare_nodes(centres, nodes):
    tiles = nodes.shape[1] // BLK
    step = 32 if tiles % 32 == 0 else tiles
    return pl.pallas_call(
        node_kernel,
        grid=(tiles // step,),
        in_specs=[
            pl.BlockSpec((3, BLK), lambda i: (0, 0)),
            pl.BlockSpec((3, step * BLK), lambda i: (0, i)),
        ],
        out_specs=pl.BlockSpec((step, DEPTH, BLK), lambda i: (i, 0, 0)),
        out_shape=jax.ShapeDtypeStruct((tiles, DEPTH, BLK), bf16),
        name="prepare_nodes",
    )(centres, nodes)


def fill_centres(out_ref, before_ref, own_ref, after_ref):
    per = own_ref.shape[1] // BLK
    origin = own_ref[0:3, 0:1]
    for k, ref in enumerate((before_ref, own_ref, after_ref)):
        points = (ref[0:3, :] - origin) * (1.0 / RADIUS)
        a, b, c = split3(augmented(points, False))
        rows = jnp.concatenate([a, a, b, b, a, c], axis=0)
        for t in range(per):
            out_ref[k * per + t] = rows[:, t * BLK : (t + 1) * BLK].astype(bf16)


def pl_reciprocal(x):
    return pltpu.reciprocal(x, approx=True)


def phi(square):
    scaled = pl_reciprocal(lax.rsqrt(jnp.maximum(square, 1e-12)))
    remain = jnp.maximum(1.0 - scaled, 0.0)
    squared = remain * remain
    return (squared * squared * (scaled + 0.25)).astype(bf16)


def clear(tiles, total):
    def one(t, carry):
        total[t] = jnp.zeros((BLK, LANES), f32)
        return carry

    lax.fori_loop(0, tiles + 1, one, 0)


def accumulate(
    unroll, together, tiles, group_count, places, members, left_ref, right_ref, weight_ref, total
):
    def step(g, carry):
        for h in range(unroll):
            group = g * unroll + h
            place = places[group]
            ids = [members[group * together + j] for j in range(together)]
            left = jnp.concatenate([left_ref[jnp.minimum(t, tiles - 1)] for t in ids], axis=1)
            square = lax.dot_general(
                left, right_ref[place], (((0,), (0,)), ((), ())), preferred_element_type=f32
            )
            image = jnp.dot(phi(square), weight_ref[place], preferred_element_type=f32)
            for j, t in enumerate(ids):
                total[t] += image[j * BLK : (j + 1) * BLK]
        return carry

    lax.fori_loop(0, group_count, step, 0)


def modes_of(ref):
    return ref[ref.shape[0] - MODES :, :]


def fill_weights(weight_ref, fields, per):
    width = 2 * MODES * len(fields[0])
    for k, refs in enumerate(fields):
        stack = jnp.concatenate([modes_of(r).astype(f32) for r in refs], axis=0) * 4.0
        high = stack.astype(bf16).astype(f32)
        low = stack - high
        rows = jnp.concatenate(
            [high, low, jnp.zeros((LANES - width, stack.shape[1]), f32)], axis=0
        )
        for t in range(per):
            weight_ref[k * per + t] = jnp.transpose(rows[:, t * BLK : (t + 1) * BLK]).astype(bf16)


def operator_kernel(unroll, together, tiles, first, count_ref, place_ref, member_ref, left_ref, *refs):
    if first:
        before_ref, own_ref, after_ref, out_ref, right_ref, weight_ref, total = refs
        fill_centres(right_ref, before_ref, own_ref, after_ref)
    else:
        right_ref, before_ref, own_ref, after_ref, out_ref, weight_ref, total = refs
    fill_weights(weight_ref, ((before_ref,), (own_ref,), (after_ref,)), tiles)
    clear(tiles, total)
    accumulate(
        unroll, together, tiles, count_ref[0], place_ref, member_ref, left_ref, right_ref,
        weight_ref, total,
    )
    own = modes_of(own_ref)
    for t in range(tiles):
        image = jnp.transpose(total[t])
        sl = slice(t * BLK, (t + 1) * BLK)
        out_ref[:, sl] = image[0:MODES] + image[MODES : 2 * MODES] + SHIFT * own[:, sl]


def apply_operator(unroll, together, lists, left, right, before, own, after):
    tiles = own.shape[1] // BLK
    vmem, smem = whole(pltpu.VMEM), whole(pltpu.SMEM)
    first = right is None
    image = jax.ShapeDtypeStruct((MODES, own.shape[1]), f32)
    factors = jax.ShapeDtypeStruct((3 * tiles, DEPTH, BLK), bf16)
    return pl.pallas_call(
        functools.partial(operator_kernel, unroll, together, tiles, first),
        in_specs=[smem] * 3 + [vmem] * (4 if first else 5),
        out_specs=(vmem, vmem) if first else vmem,
        out_shape=(image, factors) if first else image,
        scratch_shapes=[
            pltpu.VMEM((3 * tiles, BLK, LANES), bf16),
            pltpu.VMEM((tiles + 1, BLK, LANES), f32),
        ],
        compiler_params=pltpu.CompilerParams(vmem_limit_bytes=40 * 2**20),
        name="operator",
    )(*lists, left, *(() if first else (right,)), before, own, after)


def row_of(columns):
    mode = lax.broadcasted_iota(jnp.int32, (MODES, BLK), 0)
    lane = lax.broadcasted_iota(jnp.int32, (MODES, BLK), 1)
    spread = jnp.zeros((MODES, BLK), f32)
    for q, column in enumerate(columns):
        spread = jnp.where(lane == q * MODES + mode, column, spread)
    return jnp.sum(spread, axis=0, keepdims=True)


def columns_of(row, count):
    mode = lax.broadcasted_iota(jnp.int32, (MODES, BLK), 0)
    lane = lax.broadcasted_iota(jnp.int32, (MODES, BLK), 1)
    return [
        jnp.sum(jnp.where(lane == q * MODES + mode, row, 0.0), axis=1, keepdims=True)
        for q in range(count)
    ]


PAIRS = ((0, 0), (0, 1), (1, 1), (1, 2), (2, 2), (0, 2))


def volume_kernel(
    unroll, together, sizes, share, count_ref, place_ref, member_ref, turn_ref, right_ref, *refs
):
    lefts, fields = refs[0:3], (refs[3:6], refs[6:9], refs[9:12])
    out_ref, guest_ref, sums_ref, weight_ref, total, left_ref, image_ref, sems, sent = refs[12:]
    own, guests, checks = sizes
    tiles = own + guests + checks
    turn = turn_ref[0]
    spans = (
        (lefts[0], left_ref.at[pl.ds(0, own)]),
        (lefts[1], left_ref.at[pl.ds(own, guests)]),
        (lefts[2].at[pl.ds(turn * checks, checks)], left_ref.at[pl.ds(own + guests, checks)]),
    )
    copies = [pltpu.make_async_copy(a, b, sems.at[i]) for i, (a, b) in enumerate(spans)]
    for copy in copies:
        copy.start()
    per = fields[1][0].shape[1] // BLK
    fill_weights(weight_ref, fields, per)
    clear(tiles, total)
    for copy in copies:
        copy.wait()
    accumulate(
        unroll, together, tiles, count_ref[0], place_ref, member_ref, left_ref, right_ref,
        weight_ref, total,
    )
    wide = KRYLOV * MODES
    zeros = tuple(jnp.zeros((MODES, BLK), f32) for _ in PAIRS)

    def finish(first, ref, sem, steps, g, gram):
        for h in range(steps):
            t = first + g * steps + h
            image = jnp.transpose(total[t])
            image = image[0:wide] + image[wide : 2 * wide]
            image_ref[:, pl.ds(pl.multiple_of(t * BLK, BLK), BLK)] = image
            parts = [image[k * MODES : (k + 1) * MODES] for k in range(KRYLOV)]
            gram = tuple(s + parts[i] * parts[j] for s, (i, j) in zip(gram, PAIRS))
        width = steps * BLK
        start = pl.multiple_of(first * BLK + g * width, BLK)
        pltpu.make_async_copy(
            image_ref.at[:, pl.ds(start, width)],
            ref.at[:, pl.ds(pl.multiple_of(g * width, BLK), width)],
            sem,
        ).start()
        return gram

    def steps_of(count):
        return next(n for n in (8, 4, 5, 3, 2, 1) if count % n == 0)

    n = steps_of(guests)
    gram = lax.fori_loop(0, guests // n, functools.partial(finish, own, guest_ref, sent.at[1], n), zeros)
    n = steps_of(own)
    gram = lax.fori_loop(0, own // n, functools.partial(finish, 0, out_ref, sent.at[0], n), gram)
    columns = [jnp.sum(s, axis=1, keepdims=True) for s in gram]
    v = [r[...] for r in fields[1]]
    moments = [v[0] * v[0], v[0] * v[1], v[1] * v[1], v[1] * v[2], v[2] * v[2]]
    columns += [share * jnp.sum(s, axis=1, keepdims=True) for s in moments]
    last = jnp.zeros((MODES, BLK), f32)
    low = 2 * MODES
    for b in range(checks):
        image = jnp.transpose(total[own + guests + b])
        start = pl.multiple_of((turn * checks + b) * BLK, BLK)
        piece = fields[1][2][:, pl.ds(start, BLK)]
        image = image[low : low + MODES] + image[wide + low : wide + low + MODES]
        last = last + piece * (image + SHIFT * piece)
    columns.append(jnp.sum(last, axis=1, keepdims=True))
    row = row_of(columns)
    pair = jnp.concatenate([row[:, 0:LANES], row[:, LANES : 2 * LANES]], axis=0)
    sums_ref[...] = jnp.broadcast_to(pair[None], sums_ref.shape)
    pltpu.make_async_copy(image_ref.at[:, pl.ds(0, own * BLK)], out_ref, sent.at[0]).wait()
    pltpu.make_async_copy(image_ref.at[:, pl.ds(own * BLK, guests * BLK)], guest_ref, sent.at[1]).wait()


def volume_images(unroll, together, lists, turn, right, lefts, checks, fields, devices, share):
    per = fields[1][0].shape[1] // BLK
    own, guests = lefts[0].shape[0], lefts[1].shape[0]
    tiles = own + guests + checks
    vmem, smem, far = whole(pltpu.VMEM), whole(pltpu.SMEM), whole(pltpu.HBM)
    return pl.pallas_call(
        functools.partial(volume_kernel, unroll, together, (own, guests, checks), share),
        in_specs=[smem] * 4 + [vmem] + [far] * 3 + [vmem] * 9,
        out_specs=(far, far, vmem),
        out_shape=(
            jax.ShapeDtypeStruct((KRYLOV * MODES, own * BLK), f32),
            jax.ShapeDtypeStruct((KRYLOV * MODES, guests * BLK), f32),
            jax.ShapeDtypeStruct((devices, 2, LANES), f32),
        ),
        scratch_shapes=[
            pltpu.VMEM((3 * per, BLK, LANES), bf16),
            pltpu.VMEM((tiles + 1, BLK, LANES), f32),
            pltpu.VMEM((tiles, DEPTH, BLK), bf16),
            pltpu.VMEM((KRYLOV * MODES, (own + guests) * BLK), f32),
            pltpu.SemaphoreType.DMA((3,)),
            pltpu.SemaphoreType.DMA((2,)),
        ],
        compiler_params=pltpu.CompilerParams(vmem_limit_bytes=50 * 2**20),
        name="volume",
    )(*lists, turn, right, *lefts, *[f for side in fields for f in side])


def coefficients(row, total_nodes):
    columns = columns_of(row, 2 * len(PAIRS))
    gram, mu = columns[:6], columns[6:]
    zero = jnp.zeros_like(mu[0])
    one = jnp.ones_like(mu[0])

    def pairing(a, b, extra):
        out = zero
        for i, x in enumerate(a):
            for j, y in enumerate(b):
                out = out + x * y * mu[i + j + extra]
        return out

    residual, direction = [one], [one]
    answer = [zero, zero, zero]
    norm = mu[0]
    for iteration in range(KRYLOV):
        size = norm / pairing(direction, direction, 1)
        for i, x in enumerate(direction):
            answer[i] = answer[i] + size * x
        if iteration + 1 < KRYLOV:
            grown = residual + [zero]
            for i, x in enumerate(direction):
                grown[i + 1] = grown[i + 1] - size * x
            residual = grown
            later = pairing(residual, residual, 0)
            ratio = later / norm
            longer = direction + [zero]
            direction = [r + ratio * d for r, d in zip(residual, longer)]
            norm = later
    power = zero
    for s, (i, j) in zip(gram, PAIRS):
        power = power + (1.0 if i == j else 2.0) * s * answer[i] * answer[j]
    scale = jnp.sqrt(jnp.maximum(power, 0.0) / total_nodes + 1e-06)
    return answer, [a / scale for a in answer]


def settle_kernel(total_nodes, sums_ref, v0_ref, v1_ref, v2_ref, far_ref, weights_ref, coef_ref, out_ref, guest_ref, sem):
    copy = pltpu.make_async_copy(far_ref, guest_ref, sem)
    copy.start()
    pair = jnp.sum(sums_ref[...], axis=0)
    row = jnp.concatenate([pair[0:1], pair[1:2]], axis=1)
    answer, scaled = coefficients(row, total_nodes)
    weights_ref[...] = answer[0] * v0_ref[...] + answer[1] * v1_ref[...] + answer[2] * v2_ref[...]
    for k, column in enumerate(scaled):
        coef_ref[k] = jnp.broadcast_to(column, (MODES, LANES))
    copy.wait()
    out_ref[...] = blend(scaled, guest_ref).astype(bf16)


def blend(c, image_ref):
    return (
        c[0] * image_ref[0:MODES]
        + c[1] * image_ref[MODES : 2 * MODES]
        + c[2] * image_ref[2 * MODES : 3 * MODES]
    )


def settle(sums, vectors, guests, total_nodes):
    vmem = whole(pltpu.VMEM)
    return pl.pallas_call(
        functools.partial(settle_kernel, total_nodes),
        in_specs=[vmem] * 4 + [whole(pltpu.HBM)],
        out_specs=(vmem,) * 3,
        out_shape=(
            jax.ShapeDtypeStruct(vectors[0].shape, f32),
            jax.ShapeDtypeStruct((KRYLOV, MODES, LANES), f32),
            jax.ShapeDtypeStruct((MODES, guests.shape[1]), bf16),
        ),
        scratch_shapes=[pltpu.VMEM(guests.shape, f32), pltpu.SemaphoreType.DMA],
        name="settle",
    )(sums, *vectors, guests)


def combine_kernel(coef_ref, image_ref, out_ref):
    out_ref[...] = blend([coef_ref[k][:, 0:1] for k in range(KRYLOV)], image_ref)


def combine(coef, images):
    nodes = images.shape[1]
    width = 8192 if nodes % 8192 == 0 else nodes
    return pl.pallas_call(
        combine_kernel,
        grid=(nodes // width,),
        in_specs=[
            pl.BlockSpec(coef.shape, lambda i: (0, 0, 0)),
            pl.BlockSpec((KRYLOV * MODES, width), lambda i: (0, i)),
        ],
        out_specs=pl.BlockSpec((MODES, width), lambda i: (0, i)),
        out_shape=jax.ShapeDtypeStruct((MODES, nodes), f32),
        name="combine",
    )(coef, images)


def insert_kernel(kept, turn_ref, *refs):
    parts, out_ref, wide, sems = refs[1:-3], refs[-3], refs[-2], refs[-1]

    @pl.when(turn_ref[0] == 0)
    def _():
        width = parts[0].shape[1]
        copies = []
        for k, part in enumerate(parts):
            wide[k] = part[...].astype(f32)
            target = out_ref.at[:, pl.ds((kept + k * width // BLK) * BLK, width)]
            copy = pltpu.make_async_copy(wide.at[k], target, sems.at[k])
            copy.start()
            copies.append(copy)
        for copy in copies:
            copy.wait()


def insert(turn, main, parts, kept):
    vmem, far = whole(pltpu.VMEM), whole(pl.ANY)
    return pl.pallas_call(
        functools.partial(insert_kernel, kept),
        in_specs=[whole(pltpu.SMEM), far] + [vmem] * len(parts),
        out_specs=far,
        out_shape=jax.ShapeDtypeStruct(main.shape, f32),
        input_output_aliases={1: 0},
        scratch_shapes=[
            pltpu.VMEM((len(parts),) + parts[0].shape, f32),
            pltpu.SemaphoreType.DMA((len(parts),)),
        ],
        name="insert",
    )(turn, main, *parts)


def work_list(places, together, unroll, kinds):
    rows, slots = places.shape
    limit = -(-(rows * slots + kinds * (together - 1)) // together)
    limit = -(-limit // unroll) * unroll
    kind = jnp.arange(kinds, dtype=jnp.int32)
    present = jnp.any(places[:, :, None] == kind, axis=1).astype(f32)
    lower = (jnp.arange(rows)[:, None] >= jnp.arange(rows)[None, :]).astype(f32)
    reach = jnp.dot(lower, present, preferred_element_type=f32)
    groups = jnp.ceil(reach[-1] / together)
    before = (jnp.arange(kinds)[:, None] < jnp.arange(kinds)[None, :]).astype(f32)
    start = jnp.sum(before * groups[:, None], axis=0)
    end = start + groups
    index = jnp.arange(limit, dtype=jnp.int32).astype(f32)
    chosen = (index[:, None] >= start[None, :]) & (index[:, None] < end[None, :])
    place = jnp.sum(jnp.where(chosen, kind[None, :], 0), axis=1)
    first = together * (index - jnp.sum(jnp.where(chosen, start[None, :], 0.0), axis=1))
    reached = jnp.dot(chosen.astype(f32), reach.T, preferred_element_type=f32)
    rank = first[:, None] + jnp.arange(together).astype(f32)[None, :]
    member = jnp.sum((reached[:, None, :] <= rank[:, :, None]).astype(jnp.int32), axis=2)
    count = jnp.ceil(jnp.sum(groups) / unroll).astype(jnp.int32).reshape(1)
    return count, place.astype(jnp.int32), member.reshape(-1)


def neighbour_pairs(axis):
    count = lax.axis_size(axis)
    return [(i, i + 1) for i in range(count - 1)], [(i + 1, i) for i in range(count - 1)]


MOVED_SHARE = 1 / 8


def helper_turns(count):
    return (1, 2, count - 2, count - 1) if count >= 6 else (1,)


def per_device(centres, mode_shapes, neighbours, volume_nodes, supports):
    blk_dev = neighbours.shape[0]
    tile_dev, slots = supports.shape
    kinds = 3 * blk_dev
    offset = (lax.axis_index("surf") - 1) * blk_dev
    helpers = helper_turns(lax.axis_size("vol"))
    turn = lax.axis_index("vol")
    turns = turn.astype(jnp.int32).reshape(1)
    devices = lax.axis_size("surf") * lax.axis_size("vol")
    share = 1.0 / lax.axis_size("vol")
    checks = blk_dev // lax.axis_size("vol")
    total_nodes = volume_nodes.shape[1] * devices
    moved = int(tile_dev * MOVED_SHARE)
    kept = tile_dev - len(helpers) * moved

    packed = jnp.concatenate([centres, jnp.zeros((5, centres.shape[1]), f32), mode_shapes], axis=0)
    up, down = neighbour_pairs("surf")
    before = lax.ppermute(packed, "surf", up)

    def place_of(ids):
        return jnp.where(ids >= 0, jnp.clip(ids - offset, 0, kinds - 1), -1)

    own_places = place_of(neighbours)
    own_list = work_list(own_places, 3, 8, kinds)
    own_left = prepare_nodes(centres, centres)
    again, own_left, own_list = lax.optimization_barrier((packed, own_left, own_list))
    after = lax.ppermute(again, "surf", down)
    left = prepare_nodes(centres, volume_nodes)

    v0 = mode_shapes
    v1, right = apply_operator(8, 3, own_list, own_left, None, before, packed, after)
    v1_low = v1.astype(bf16)
    v1_before = lax.ppermute(v1_low, "surf", up)
    v1_after = lax.ppermute(v1_low, "surf", down)

    ids = jnp.pad(supports[kept:].astype(f32), ((0, 0), (0, BLK - slots))).reshape(1, -1)
    parcel = jnp.concatenate([volume_nodes[:, kept * BLK :], ids], axis=0)
    parcel, v1_before = lax.optimization_barrier((parcel, v1_before))
    width = moved * BLK
    got = jnp.zeros((4, width), f32)
    helping = False
    for k, helper in enumerate(helpers):
        piece = parcel[:, k * width : (k + 1) * width]
        got = got + lax.ppermute(piece, "vol", [(0, helper)])
        helping = helping | (turn == helper)
    v2 = apply_operator(8, 3, own_list, own_left, right, v1_before, v1, v1_after)
    v2_low = v2.astype(bf16)
    v2_before = lax.ppermute(v2_low, "surf", up)
    v2_after = lax.ppermute(v2_low, "surf", down)
    guest_left = prepare_nodes(centres, got[:3])

    guest_ids = got[3].reshape(moved, BLK)[:, :slots].astype(jnp.int32)
    guest_places = jnp.where(helping, place_of(guest_ids), -1)
    kept_here = (turn > 0) | (jnp.arange(tile_dev) < kept)
    tile_places = jnp.where(kept_here[:, None], place_of(supports), -1)
    check_places = lax.dynamic_slice_in_dim(own_places, turn * checks, checks, axis=0)
    places = jnp.concatenate([tile_places, guest_places, check_places], axis=0)
    whole_list = work_list(places, 2, 10, kinds)
    fields = (
        (before, v1_before, v2_before),
        (v0, v1, v2),
        (after, v1_after, v2_after),
    )
    lefts = (left, guest_left, own_left)
    images, guests, sums = volume_images(
        10, 2, whole_list, turns, right, lefts, checks, fields, devices, share
    )
    sums = lax.all_to_all(sums, ("surf", "vol"), 0, 0, tiled=True)
    weights, coef, away = settle(sums, (v0, v1, v2), guests, total_nodes)
    parts = [lax.ppermute(away, "vol", [(helper, 0)]) for helper in helpers]
    return weights, insert(turns, combine(coef, images), parts, kept)


def solution(mesh):
    return jax.shard_map(
        per_device,
        mesh=mesh,
        in_specs=(
            P(None, "surf"),
            P(None, "surf"),
            P("surf", None),
            P(None, ("surf", "vol")),
            P(("surf", "vol"), None),
        ),
        out_specs=(P(None, "surf"), P(None, ("surf", "vol"))),
        check_vma=False,
    )
```

```python
import functools

import jax
import jax.numpy as jnp
from jax import lax
from jax.experimental import pallas as pl
from jax.experimental.pallas import tpu as pltpu
from jax.sharding import PartitionSpec as P

MODES = 16
BLK = 256
RADIUS = 0.9
SHIFT = 0.5
DEPTH = 48
KRYLOV = 3
LANES = 128
f32 = jnp.float32
bf16 = jnp.bfloat16


def whole(memory):
    return pl.BlockSpec(memory_space=memory)


def split3(x):
    first = x.astype(bf16).astype(f32)
    rest = x - first
    second = rest.astype(bf16).astype(f32)
    return first, second, rest - second


def augmented(points, is_node):
    count = points.shape[1]
    row = lax.broadcasted_iota(jnp.int32, (8, count), 0)
    square = jnp.sum(points * points, axis=0, keepdims=True)
    one = jnp.ones_like(square)
    if is_node:
        coords, low, high = points, square, one
    else:
        coords, low, high = -2.0 * points, one, square
    zeros = jnp.zeros((5, count), f32)
    padded = jnp.concatenate([coords, zeros], axis=0)
    return jnp.where(row == 3, low, jnp.where(row == 4, high, padded))


def node_kernel(centres_ref, nodes_ref, out_ref):
    points = (nodes_ref[...] - centres_ref[:, 0:1]) * (1.0 / RADIUS)
    a, b, c = split3(augmented(points, True))
    rows = jnp.concatenate([a, b, a, b, c, a], axis=0)
    for t in range(out_ref.shape[0]):
        out_ref[t] = rows[:, t * BLK : (t + 1) * BLK].astype(bf16)


def prepare_nodes(centres, nodes):
    tiles = nodes.shape[1] // BLK
    step = 64 if tiles % 64 == 0 else tiles
    return pl.pallas_call(
        node_kernel,
        grid=(tiles // step,),
        in_specs=[
            pl.BlockSpec((3, BLK), lambda i: (0, 0)),
            pl.BlockSpec((3, step * BLK), lambda i: (0, i)),
        ],
        out_specs=pl.BlockSpec((step, DEPTH, BLK), lambda i: (i, 0, 0)),
        out_shape=jax.ShapeDtypeStruct((tiles, DEPTH, BLK), bf16),
        compiler_params=pltpu.CompilerParams(vmem_limit_bytes=32 * 2**20),
        name="prepare_nodes",
    )(centres, nodes)


def fill_centres(out_ref, before_ref, own_ref, after_ref):
    per = own_ref.shape[1] // BLK
    origin = own_ref[0:3, 0:1]
    for k, ref in enumerate((before_ref, own_ref, after_ref)):
        points = (ref[0:3, :] - origin) * (1.0 / RADIUS)
        a, b, c = split3(augmented(points, False))
        rows = jnp.concatenate([a, a, b, b, a, c], axis=0)
        for t in range(per):
            out_ref[k * per + t] = rows[:, t * BLK : (t + 1) * BLK].astype(bf16)


def pl_reciprocal(x):
    return pltpu.reciprocal(x, approx=True)


def phi(square):
    scaled = pl_reciprocal(lax.rsqrt(jnp.maximum(square, 1e-12)))
    remain = jnp.maximum(1.0 - scaled, 0.0)
    squared = remain * remain
    return (squared * squared * (scaled + 0.25)).astype(bf16)


def clear(tiles, total):
    def one(t, carry):
        total[t] = jnp.zeros((BLK, LANES), f32)
        return carry

    lax.fori_loop(0, tiles + 1, one, 0)


def accumulate(
    unroll, together, tiles, group_count, places, members, left_ref, right_ref, weight_ref, total
):
    def step(g, carry):
        for h in range(unroll):
            group = g * unroll + h
            place = places[group]
            ids = [members[group * together + j] for j in range(together)]
            left = jnp.concatenate([left_ref[jnp.minimum(t, tiles - 1)] for t in ids], axis=1)
            square = lax.dot_general(
                left, right_ref[place], (((0,), (0,)), ((), ())), preferred_element_type=f32
            )
            image = jnp.dot(phi(square), weight_ref[place], preferred_element_type=f32)
            for j, t in enumerate(ids):
                total[t] += image[j * BLK : (j + 1) * BLK]
        return carry

    lax.fori_loop(0, group_count, step, 0)


def modes_of(ref):
    return ref[ref.shape[0] - MODES :, :]


def fill_weights(weight_ref, fields, per):
    width = 2 * MODES * len(fields[0])
    for k, refs in enumerate(fields):
        stack = jnp.concatenate([modes_of(r).astype(f32) for r in refs], axis=0) * 4.0
        high = stack.astype(bf16).astype(f32)
        low = stack - high
        rows = jnp.concatenate(
            [high, low, jnp.zeros((LANES - width, stack.shape[1]), f32)], axis=0
        )
        for t in range(per):
            weight_ref[k * per + t] = jnp.transpose(rows[:, t * BLK : (t + 1) * BLK]).astype(bf16)


def operator_kernel(unroll, together, tiles, first, count_ref, place_ref, member_ref, left_ref, *refs):
    if first:
        before_ref, own_ref, after_ref, out_ref, right_ref, weight_ref, total = refs
        fill_centres(right_ref, before_ref, own_ref, after_ref)
    else:
        right_ref, before_ref, own_ref, after_ref, out_ref, weight_ref, total = refs
    fill_weights(weight_ref, ((before_ref,), (own_ref,), (after_ref,)), tiles)
    clear(tiles, total)
    accumulate(
        unroll, together, tiles, count_ref[0], place_ref, member_ref, left_ref, right_ref,
        weight_ref, total,
    )
    own = modes_of(own_ref)
    for t in range(tiles):
        image = jnp.transpose(total[t])
        sl = slice(t * BLK, (t + 1) * BLK)
        out_ref[:, sl] = image[0:MODES] + image[MODES : 2 * MODES] + SHIFT * own[:, sl]


def apply_operator(unroll, together, lists, left, right, before, own, after):
    tiles = own.shape[1] // BLK
    vmem, smem = whole(pltpu.VMEM), whole(pltpu.SMEM)
    first = right is None
    image = jax.ShapeDtypeStruct((MODES, own.shape[1]), f32)
    factors = jax.ShapeDtypeStruct((3 * tiles, DEPTH, BLK), bf16)
    return pl.pallas_call(
        functools.partial(operator_kernel, unroll, together, tiles, first),
        in_specs=[smem] * 3 + [vmem] * (4 if first else 5),
        out_specs=(vmem, vmem) if first else vmem,
        out_shape=(image, factors) if first else image,
        scratch_shapes=[
            pltpu.VMEM((3 * tiles, BLK, LANES), bf16),
            pltpu.VMEM((tiles + 1, BLK, LANES), f32),
        ],
        compiler_params=pltpu.CompilerParams(vmem_limit_bytes=40 * 2**20),
        name="operator",
    )(*lists, left, *(() if first else (right,)), before, own, after)


def row_of(columns):
    mode = lax.broadcasted_iota(jnp.int32, (MODES, BLK), 0)
    lane = lax.broadcasted_iota(jnp.int32, (MODES, BLK), 1)
    spread = jnp.zeros((MODES, BLK), f32)
    for q, column in enumerate(columns):
        spread = jnp.where(lane == q * MODES + mode, column, spread)
    return jnp.sum(spread, axis=0, keepdims=True)


def columns_of(row, count):
    mode = lax.broadcasted_iota(jnp.int32, (MODES, BLK), 0)
    lane = lax.broadcasted_iota(jnp.int32, (MODES, BLK), 1)
    return [
        jnp.sum(jnp.where(lane == q * MODES + mode, row, 0.0), axis=1, keepdims=True)
        for q in range(count)
    ]


PAIRS = ((0, 0), (0, 1), (1, 1), (1, 2), (2, 2), (0, 2))


def volume_kernel(
    unroll, together, sizes, share, count_ref, place_ref, member_ref, turn_ref, right_ref, *refs
):
    lefts, fields = refs[0:3], (refs[3:6], refs[6:9], refs[9:12])
    out_ref, guest_ref, sums_ref, weight_ref, total, left_ref, image_ref, sems, sent = refs[12:]
    own, guests, checks = sizes
    tiles = own + guests + checks
    turn = turn_ref[0]
    spans = (
        (lefts[0], left_ref.at[pl.ds(0, own)]),
        (lefts[1], left_ref.at[pl.ds(own, guests)]),
        (lefts[2].at[pl.ds(turn * checks, checks)], left_ref.at[pl.ds(own + guests, checks)]),
    )
    copies = [pltpu.make_async_copy(a, b, sems.at[i]) for i, (a, b) in enumerate(spans)]
    for copy in copies:
        copy.start()
    per = fields[1][0].shape[1] // BLK
    fill_weights(weight_ref, fields, per)
    clear(tiles, total)
    for copy in copies:
        copy.wait()
    accumulate(
        unroll, together, tiles, count_ref[0], place_ref, member_ref, left_ref, right_ref,
        weight_ref, total,
    )
    wide = KRYLOV * MODES
    zeros = tuple(jnp.zeros((MODES, BLK), f32) for _ in PAIRS)

    def finish(first, ref, sem, steps, g, gram):
        for h in range(steps):
            t = first + g * steps + h
            image = jnp.transpose(total[t])
            image = image[0:wide] + image[wide : 2 * wide]
            image_ref[:, pl.ds(pl.multiple_of(t * BLK, BLK), BLK)] = image
            parts = [image[k * MODES : (k + 1) * MODES] for k in range(KRYLOV)]
            gram = tuple(s + parts[i] * parts[j] for s, (i, j) in zip(gram, PAIRS))
        width = steps * BLK
        start = pl.multiple_of(first * BLK + g * width, BLK)
        pltpu.make_async_copy(
            image_ref.at[:, pl.ds(start, width)],
            ref.at[:, pl.ds(pl.multiple_of(g * width, BLK), width)],
            sem,
        ).start()
        return gram

    def steps_of(count):
        return next(n for n in (8, 4, 5, 3, 2, 1) if count % n == 0)

    n = steps_of(guests)
    gram = lax.fori_loop(0, guests // n, functools.partial(finish, own, guest_ref, sent.at[1], n), zeros)
    n = steps_of(own)
    gram = lax.fori_loop(0, own // n, functools.partial(finish, 0, out_ref, sent.at[0], n), gram)
    columns = [jnp.sum(s, axis=1, keepdims=True) for s in gram]
    v = [r[...] for r in fields[1]]
    moments = [v[0] * v[0], v[0] * v[1], v[1] * v[1], v[1] * v[2], v[2] * v[2]]
    columns += [share * jnp.sum(s, axis=1, keepdims=True) for s in moments]
    last = jnp.zeros((MODES, BLK), f32)
    low = 2 * MODES
    for b in range(checks):
        image = jnp.transpose(total[own + guests + b])
        start = pl.multiple_of((turn * checks + b) * BLK, BLK)
        piece = fields[1][2][:, pl.ds(start, BLK)]
        image = image[low : low + MODES] + image[wide + low : wide + low + MODES]
        last = last + piece * (image + SHIFT * piece)
    columns.append(jnp.sum(last, axis=1, keepdims=True))
    row = row_of(columns)
    pair = jnp.concatenate([row[:, 0:LANES], row[:, LANES : 2 * LANES]], axis=0)
    sums_ref[...] = jnp.broadcast_to(pair[None], sums_ref.shape)
    pltpu.make_async_copy(image_ref.at[:, pl.ds(0, own * BLK)], out_ref, sent.at[0]).wait()
    pltpu.make_async_copy(image_ref.at[:, pl.ds(own * BLK, guests * BLK)], guest_ref, sent.at[1]).wait()


def volume_images(unroll, together, lists, turn, right, lefts, checks, fields, devices, share):
    per = fields[1][0].shape[1] // BLK
    own, guests = lefts[0].shape[0], lefts[1].shape[0]
    tiles = own + guests + checks
    vmem, smem, far = whole(pltpu.VMEM), whole(pltpu.SMEM), whole(pltpu.HBM)
    return pl.pallas_call(
        functools.partial(volume_kernel, unroll, together, (own, guests, checks), share),
        in_specs=[smem] * 4 + [vmem] + [far] * 3 + [vmem] * 9,
        out_specs=(far, far, vmem),
        out_shape=(
            jax.ShapeDtypeStruct((KRYLOV * MODES, own * BLK), f32),
            jax.ShapeDtypeStruct((KRYLOV * MODES, guests * BLK), f32),
            jax.ShapeDtypeStruct((devices, 2, LANES), f32),
        ),
        scratch_shapes=[
            pltpu.VMEM((3 * per, BLK, LANES), bf16),
            pltpu.VMEM((tiles + 1, BLK, LANES), f32),
            pltpu.VMEM((tiles, DEPTH, BLK), bf16),
            pltpu.VMEM((KRYLOV * MODES, (own + guests) * BLK), f32),
            pltpu.SemaphoreType.DMA((3,)),
            pltpu.SemaphoreType.DMA((2,)),
        ],
        compiler_params=pltpu.CompilerParams(vmem_limit_bytes=50 * 2**20),
        name="volume",
    )(*lists, turn, right, *lefts, *[f for side in fields for f in side])


def coefficients(row, total_nodes):
    columns = columns_of(row, 2 * len(PAIRS))
    gram, mu = columns[:6], columns[6:]
    zero = jnp.zeros_like(mu[0])
    one = jnp.ones_like(mu[0])

    def pairing(a, b, extra):
        out = zero
        for i, x in enumerate(a):
            for j, y in enumerate(b):
                out = out + x * y * mu[i + j + extra]
        return out

    residual, direction = [one], [one]
    answer = [zero, zero, zero]
    norm = mu[0]
    for iteration in range(KRYLOV):
        size = norm / pairing(direction, direction, 1)
        for i, x in enumerate(direction):
            answer[i] = answer[i] + size * x
        if iteration + 1 < KRYLOV:
            grown = residual + [zero]
            for i, x in enumerate(direction):
                grown[i + 1] = grown[i + 1] - size * x
            residual = grown
            later = pairing(residual, residual, 0)
            ratio = later / norm
            longer = direction + [zero]
            direction = [r + ratio * d for r, d in zip(residual, longer)]
            norm = later
    power = zero
    for s, (i, j) in zip(gram, PAIRS):
        power = power + (1.0 if i == j else 2.0) * s * answer[i] * answer[j]
    scale = jnp.sqrt(jnp.maximum(power, 0.0) / total_nodes + 1e-06)
    return answer, [a / scale for a in answer]


def settle_kernel(total_nodes, sums_ref, v0_ref, v1_ref, v2_ref, far_ref, weights_ref, coef_ref, out_ref, guest_ref, sem):
    copy = pltpu.make_async_copy(far_ref, guest_ref, sem)
    copy.start()
    pair = jnp.sum(sums_ref[...], axis=0)
    row = jnp.concatenate([pair[0:1], pair[1:2]], axis=1)
    answer, scaled = coefficients(row, total_nodes)
    weights_ref[...] = answer[0] * v0_ref[...] + answer[1] * v1_ref[...] + answer[2] * v2_ref[...]
    for k, column in enumerate(scaled):
        coef_ref[k] = jnp.broadcast_to(column, (MODES, LANES))
    copy.wait()
    out_ref[...] = blend(scaled, guest_ref).astype(bf16)


def blend(c, image_ref):
    return (
        c[0] * image_ref[0:MODES]
        + c[1] * image_ref[MODES : 2 * MODES]
        + c[2] * image_ref[2 * MODES : 3 * MODES]
    )


def settle(sums, vectors, guests, total_nodes):
    vmem = whole(pltpu.VMEM)
    return pl.pallas_call(
        functools.partial(settle_kernel, total_nodes),
        in_specs=[vmem] * 4 + [whole(pltpu.HBM)],
        out_specs=(vmem,) * 3,
        out_shape=(
            jax.ShapeDtypeStruct(vectors[0].shape, f32),
            jax.ShapeDtypeStruct((KRYLOV, MODES, LANES), f32),
            jax.ShapeDtypeStruct((MODES, guests.shape[1]), bf16),
        ),
        scratch_shapes=[pltpu.VMEM(guests.shape, f32), pltpu.SemaphoreType.DMA],
        name="settle",
    )(sums, *vectors, guests)


def combine_kernel(coef_ref, image_ref, out_ref):
    out_ref[...] = blend([coef_ref[k][:, 0:1] for k in range(KRYLOV)], image_ref)


def combine(coef, images):
    nodes = images.shape[1]
    width = 16384 if nodes % 16384 == 0 else nodes
    return pl.pallas_call(
        combine_kernel,
        grid=(nodes // width,),
        in_specs=[
            pl.BlockSpec(coef.shape, lambda i: (0, 0, 0)),
            pl.BlockSpec((KRYLOV * MODES, width), lambda i: (0, i)),
        ],
        out_specs=pl.BlockSpec((MODES, width), lambda i: (0, i)),
        out_shape=jax.ShapeDtypeStruct((MODES, nodes), f32),
        compiler_params=pltpu.CompilerParams(vmem_limit_bytes=24 * 2**20),
        name="combine",
    )(coef, images)


def insert_kernel(kept, turn_ref, *refs):
    parts, out_ref, wide, sems = refs[1:-3], refs[-3], refs[-2], refs[-1]

    @pl.when(turn_ref[0] == 0)
    def _():
        width = parts[0].shape[1]
        copies = []
        for k, part in enumerate(parts):
            wide[k] = part[...].astype(f32)
            target = out_ref.at[:, pl.ds((kept + k * width // BLK) * BLK, width)]
            copy = pltpu.make_async_copy(wide.at[k], target, sems.at[k])
            copy.start()
            copies.append(copy)
        for copy in copies:
            copy.wait()


def insert(turn, main, parts, kept):
    vmem, far = whole(pltpu.VMEM), whole(pl.ANY)
    return pl.pallas_call(
        functools.partial(insert_kernel, kept),
        in_specs=[whole(pltpu.SMEM), far] + [vmem] * len(parts),
        out_specs=far,
        out_shape=jax.ShapeDtypeStruct(main.shape, f32),
        input_output_aliases={1: 0},
        scratch_shapes=[
            pltpu.VMEM((len(parts),) + parts[0].shape, f32),
            pltpu.SemaphoreType.DMA((len(parts),)),
        ],
        name="insert",
    )(turn, main, *parts)


def work_list(places, together, unroll, kinds):
    rows, slots = places.shape
    limit = -(-(rows * slots + kinds * (together - 1)) // together)
    limit = -(-limit // unroll) * unroll
    kind = jnp.arange(kinds, dtype=jnp.int32)
    present = jnp.any(places[:, :, None] == kind, axis=1).astype(f32)
    lower = (jnp.arange(rows)[:, None] >= jnp.arange(rows)[None, :]).astype(f32)
    reach = jnp.dot(lower, present, preferred_element_type=f32)
    groups = jnp.ceil(reach[-1] / together)
    before = (jnp.arange(kinds)[:, None] < jnp.arange(kinds)[None, :]).astype(f32)
    start = jnp.sum(before * groups[:, None], axis=0)
    end = start + groups
    index = jnp.arange(limit, dtype=jnp.int32).astype(f32)
    chosen = (index[:, None] >= start[None, :]) & (index[:, None] < end[None, :])
    place = jnp.sum(jnp.where(chosen, kind[None, :], 0), axis=1)
    first = together * (index - jnp.sum(jnp.where(chosen, start[None, :], 0.0), axis=1))
    reached = jnp.dot(chosen.astype(f32), reach.T, preferred_element_type=f32)
    rank = first[:, None] + jnp.arange(together).astype(f32)[None, :]
    member = jnp.sum((reached[:, None, :] <= rank[:, :, None]).astype(jnp.int32), axis=2)
    count = jnp.ceil(jnp.sum(groups) / unroll).astype(jnp.int32).reshape(1)
    return count, place.astype(jnp.int32), member.reshape(-1)


def neighbour_pairs(axis):
    count = lax.axis_size(axis)
    return [(i, i + 1) for i in range(count - 1)], [(i + 1, i) for i in range(count - 1)]


MOVED_SHARE = 1 / 8


def helper_turns(count):
    return (1, 2, count - 2, count - 1) if count >= 6 else (1,)


def per_device(centres, mode_shapes, neighbours, volume_nodes, supports):
    blk_dev = neighbours.shape[0]
    tile_dev, slots = supports.shape
    kinds = 3 * blk_dev
    offset = (lax.axis_index("surf") - 1) * blk_dev
    helpers = helper_turns(lax.axis_size("vol"))
    turn = lax.axis_index("vol")
    turns = turn.astype(jnp.int32).reshape(1)
    devices = lax.axis_size("surf") * lax.axis_size("vol")
    share = 1.0 / lax.axis_size("vol")
    checks = blk_dev // lax.axis_size("vol")
    total_nodes = volume_nodes.shape[1] * devices
    moved = int(tile_dev * MOVED_SHARE)
    kept = tile_dev - len(helpers) * moved

    packed = jnp.concatenate([centres, jnp.zeros((5, centres.shape[1]), f32), mode_shapes], axis=0)
    up, down = neighbour_pairs("surf")
    before = lax.ppermute(packed, "surf", up)

    def place_of(ids):
        return jnp.where(ids >= 0, jnp.clip(ids - offset, 0, kinds - 1), -1)

    own_places = place_of(neighbours)
    own_list = work_list(own_places, 3, 8, kinds)
    own_left = prepare_nodes(centres, centres)
    again, own_left, own_list = lax.optimization_barrier((packed, own_left, own_list))
    after = lax.ppermute(again, "surf", down)
    left = prepare_nodes(centres, volume_nodes)

    v0 = mode_shapes
    v1, right = apply_operator(8, 3, own_list, own_left, None, before, packed, after)
    v1_low = v1.astype(bf16)
    v1_before = lax.ppermute(v1_low, "surf", up)
    v1_after = lax.ppermute(v1_low, "surf", down)

    ids = jnp.pad(supports[kept:].astype(f32), ((0, 0), (0, BLK - slots))).reshape(1, -1)
    parcel = jnp.concatenate([volume_nodes[:, kept * BLK :], ids], axis=0)
    parcel, v1_before = lax.optimization_barrier((parcel, v1_before))
    width = moved * BLK
    got = jnp.zeros((4, width), f32)
    helping = False
    for k, helper in enumerate(helpers):
        piece = parcel[:, k * width : (k + 1) * width]
        got = got + lax.ppermute(piece, "vol", [(0, helper)])
        helping = helping | (turn == helper)
    v2 = apply_operator(8, 3, own_list, own_left, right, v1_before, v1, v1_after)
    v2_low = v2.astype(bf16)
    v2_before = lax.ppermute(v2_low, "surf", up)
    v2_after = lax.ppermute(v2_low, "surf", down)
    guest_left = prepare_nodes(centres, got[:3])

    guest_ids = got[3].reshape(moved, BLK)[:, :slots].astype(jnp.int32)
    guest_places = jnp.where(helping, place_of(guest_ids), -1)
    kept_here = (turn > 0) | (jnp.arange(tile_dev) < kept)
    tile_places = jnp.where(kept_here[:, None], place_of(supports), -1)
    check_places = lax.dynamic_slice_in_dim(own_places, turn * checks, checks, axis=0)
    places = jnp.concatenate([tile_places, guest_places, check_places], axis=0)
    whole_list = work_list(places, 2, 16, kinds)
    fields = (
        (before, v1_before, v2_before),
        (v0, v1, v2),
        (after, v1_after, v2_after),
    )
    lefts = (left, guest_left, own_left)
    images, guests, sums = volume_images(
        16, 2, whole_list, turns, right, lefts, checks, fields, devices, share
    )
    sums = lax.all_to_all(sums, ("surf", "vol"), 0, 0, tiled=True)
    weights, coef, away = settle(sums, (v0, v1, v2), guests, total_nodes)
    parts = [lax.ppermute(away, "vol", [(helper, 0)]) for helper in helpers]
    return weights, insert(turns, combine(coef, images), parts, kept)


def solution(mesh):
    return jax.shard_map(
        per_device,
        mesh=mesh,
        in_specs=(
            P(None, "surf"),
            P(None, "surf"),
            P("surf", None),
            P(None, ("surf", "vol")),
            P(("surf", "vol"), None),
        ),
        out_specs=(P(None, "surf"), P(None, ("surf", "vol"))),
        check_vma=False,
    )
```
